512 devices in a mesh: ex: 16 (over x_hi, y, core), dim: 32 (over z, x_lo).
Axes of the slice: x: 4 (x_hi: 2, x_lo: 2; x = x_hi * 2 + x_lo), y: 4, z: 16, core: 2. Of those that a mesh axis runs over, the one named last changes fastest.
Arguments:
- query_grads: bfloat16 [1024, 65536], P('ex', 'dim'), may hold values from -6 to 6
- precond: bfloat16 [32, 2048, 2048], P('dim', None, 'ex'), may hold values from -0.125 to 0.125
- codes: bfloat16 [16384, 65536], P('ex', 'dim'), may hold values from -1 to 1
- scales: float32 [16384, 512], P('ex', 'dim'), may hold values from 0.2 to 2
Outputs:
- scores: float32 [1024, 16384], P('dim', 'ex')
The draws below stay inside these ranges and needn't reach their ends.
All inputs are finite; a program needn't handle non-finite values.
Results may differ from the reference program's by a relative error of at most 0.0041.
Values may be sent and summed in bfloat16 or wider, within the bound.
No kernel may reach another device: no remote copies, remote signals or barrier semaphores. Data moves between devices by JAX's collectives and lax.ppermute only.
A program may use at most 64 MiB of HBM per device.

```python
import math
import jax
import jax.numpy as jnp
from jax import lax

H = 2048
BLOCK = 128
LAYERS = 32
PROJ = 65536
QUERIES = 1024
EXAMPLES = 16384


def level_of(own_key, dims, cuts, low, high):
    factor_of = 1.0
    for position, shards_of in cuts:
        steps = jax.random.uniform(jax.random.fold_in(jax.random.fold_in(own_key, 6), position), (shards_of,), jnp.float32, low / len(cuts), high / len(cuts))
        factor_of = factor_of * jnp.repeat(jnp.exp(steps), dims[position] // shards_of).reshape((-1,) + (1,) * (len(dims) - 1 - position))
    return factor_of


def normal_values(rng, extent, scale, bound, cuts=(), held_as=jnp.bfloat16):
    level = level_of(rng, extent, cuts, -0.22, 0.18) if cuts else 1.0
    entries = jax.random.normal(rng, extent, jnp.float32) * scale * level
    return jnp.minimum(jnp.maximum(entries, -bound), bound).astype(held_as)


def setup_inputs(seed: int = 0) -> dict:
    key_of = jax.random.split(jax.random.key(seed), 5)
    return {
        "query_grads": normal_values(key_of[0], (QUERIES, PROJ), 1.0, 6.0, ((0, 16), (1, 32))),
        "precond": normal_values(key_of[1], (LAYERS, H, H), H ** -0.5, 0.125, ((0, 32), (2, 16))),
        "codes": jnp.clip(jax.random.uniform(key_of[2], (EXAMPLES, PROJ), jnp.float32, -1.0, 1.0) * level_of(key_of[2], (EXAMPLES, PROJ), ((0, 16), (1, 32)), -0.4, 0.0), -1.0, 1.0).astype(jnp.bfloat16),
        "scales": jnp.clip(jnp.exp(math.log(2.0) - 2.3025851 * jax.random.uniform(key_of[3], (EXAMPLES, PROJ // BLOCK), jnp.float32) ** level_of(key_of[3], (EXAMPLES, PROJ // BLOCK), ((0, 16), (1, 32)), -0.2, 0.2)), 0.2, 2.0),
    }


def reference(query_grads, precond, codes, scales):
    def one_layer(total, layer):
        start = (layer * H).astype(jnp.int32)
        grads_part = lax.dynamic_slice_in_dim(query_grads, start, H, 1)
        conditioned = jnp.dot(grads_part, precond[layer], preferred_element_type=jnp.float32).astype(jnp.bfloat16)
        code_part = lax.dynamic_slice_in_dim(codes, start, H, 1).astype(jnp.float32)
        scale_part = lax.dynamic_slice_in_dim(scales, (layer * (H // BLOCK)).astype(jnp.int32), H // BLOCK, 1)
        dequantized = (code_part.reshape(EXAMPLES, H // BLOCK, BLOCK) * scale_part[:, :, None]).reshape(EXAMPLES, H).astype(jnp.bfloat16)
        term = lax.dot_general(conditioned, dequantized, (((1,), (1,)), ((), ())), preferred_element_type=jnp.float32)
        return total + term, None

    start_total = jnp.zeros((QUERIES, EXAMPLES), jnp.float32)
    total, unused = lax.scan(one_layer, start_total, jnp.arange(LAYERS, dtype=jnp.int32))
    return total * (float(PROJ) ** -0.5)
```

```python
import jax
import jax.numpy as jnp
from jax import lax
from jax.sharding import PartitionSpec as P

CORES, ROWS_Y, ROWS_X = 2, 4, 2
NEAR, FAR = 4, 8


def shards(query_grads, precond, codes, scales):
    own_queries, width = query_grads.shape
    own_columns = precond.shape[2]
    examples, blocks = scales.shape
    ex_size = lax.axis_size("ex")
    slots = FAR * NEAR
    tile = own_queries * ex_size // slots // CORES
    chips = ROWS_X * ROWS_Y
    block_rows = own_queries * ROWS_Y
    place = lax.axis_index("ex")
    core, x_hi = place % CORES, place // (ROWS_Y * CORES)
    core_swap = [(e, e ^ 1) for e in range(ex_size)]
    x_swap = [(e, e ^ (ROWS_Y * CORES)) for e in range(ex_size)]
    beside = [[x * ROWS_Y * CORES + i for i in range(ROWS_Y * CORES)] for x in range(ROWS_X)]
    same_core = [[chip * CORES + c for chip in range(chips)] for c in range(CORES)]
    near = [[far * NEAR + i for i in range(NEAR)] for far in range(FAR)]
    far = [
        [(chip * CORES + c) * slots + f * NEAR + i for f in range(FAR) for c in range(CORES)]
        for chip in range(chips)
        for i in range(NEAR)
    ]

    halves = query_grads.reshape(2, CORES, tile, width).transpose(1, 0, 2, 3)
    halves = jnp.broadcast_to(halves[None], (ROWS_Y, CORES, 2, tile, width))
    grads = lax.all_to_all(
        halves.reshape(ROWS_Y * CORES, 2 * tile, width),
        "ex", 0, 0, tiled=True, axis_index_groups=beside,
    ).reshape(block_rows, width)

    own = precond[0]
    across = lax.ppermute(own, "ex", x_swap)
    both = jnp.stack([jnp.where(x_hi == 0, own, across), jnp.where(x_hi == 0, across, own)])
    other = lax.ppermute(both, "ex", core_swap)
    first, second = jnp.where(core == 0, both, other), jnp.where(core == 0, other, both)
    weights = jnp.concatenate([first[0], second[0], first[1], second[1]], axis=1)

    expanded = codes.astype(jnp.float32).reshape(examples, blocks, width // blocks)
    mine = (expanded * scales[:, :, None]).reshape(examples, width).astype(jnp.bfloat16)
    theirs = lax.ppermute(mine, "ex", core_swap)
    store = jnp.concatenate(
        [jnp.where(core == 0, mine, theirs), jnp.where(core == 0, theirs, mine)], axis=0
    )

    part = jnp.dot(grads, weights, preferred_element_type=jnp.float32).astype(jnp.bfloat16)
    parts = lax.all_to_all(
        jnp.broadcast_to(part[None], (chips,) + part.shape),
        "ex", 0, 0, tiled=True, axis_index_groups=same_core,
    )
    pair = CORES * own_columns
    conditioned = (
        parts.reshape(ROWS_X, ROWS_Y, ROWS_Y, NEAR, tile, ROWS_X, pair)
        .transpose(3, 0, 2, 4, 5, 1, 6)
        .reshape(slots * tile, width)
    )

    term = lax.dot_general(
        conditioned, store, (((1,), (1,)), ((), ())), preferred_element_type=jnp.float32
    ).astype(jnp.bfloat16)
    terms = lax.all_to_all(
        term.reshape(NEAR, FAR * tile, CORES * examples),
        "dim", 0, 0, tiled=True, axis_index_groups=near,
    )
    layers = (
        jnp.sum(terms.astype(jnp.float32), axis=0)
        .astype(jnp.bfloat16)
        .reshape(FAR, tile, CORES, examples)
        .transpose(0, 2, 1, 3)
        .reshape(FAR * CORES, tile, examples)
    )
    sums = lax.all_to_all(layers, ("ex", "dim"), 0, 0, tiled=True, axis_index_groups=far)
    total = jnp.sum(sums.astype(jnp.float32).reshape(FAR, CORES * tile, examples), axis=0)
    return total * float(width * lax.axis_size("dim")) ** (-0.5)


def solution(mesh):
    placed = (P("ex", "dim"), P("dim", None, "ex"), P("ex", "dim"), P("ex", "dim"))
    return jax.shard_map(
        shards, mesh=mesh, in_specs=placed, out_specs=P("dim", "ex"), check_vma=False
    )
```

```python
import jax
import jax.numpy as jnp
from jax import lax
from jax.experimental import pallas as pl
from jax.experimental.pallas import tpu as pltpu
from jax.sharding import PartitionSpec as P

CORES, ROWS_Y, ROWS_X = 2, 4, 2
PAIRS, SIDES = 8, 2
NEAR = 2 * SIDES
MIB = 1 << 20


def dequantize(codes_ref, scales_ref, out_ref):
    block = codes_ref.shape[1] // scales_ref.shape[1]
    for b in range(scales_ref.shape[1]):
        columns = slice(b * block, (b + 1) * block)
        entries = codes_ref[:, columns].astype(jnp.float32) * scales_ref[:, b : b + 1]
        out_ref[:, columns] = entries.astype(out_ref.dtype)


def dequantized(codes, scales):
    rows, width = codes.shape
    tile = 256
    return pl.pallas_call(
        dequantize,
        grid=(rows // tile,),
        in_specs=[
            pl.BlockSpec((tile, width), lambda r: (r, 0)),
            pl.BlockSpec((tile, scales.shape[1]), lambda r: (r, 0)),
        ],
        out_specs=pl.BlockSpec((tile, width), lambda r: (r, 0)),
        out_shape=jax.ShapeDtypeStruct(codes.shape, jnp.bfloat16),
        compiler_params=pltpu.CompilerParams(vmem_limit_bytes=24 * MIB),
        cost_estimate=pl.CostEstimate(
            flops=rows * width, bytes_accessed=4 * rows * width, transcendentals=0
        ),
    )(codes, scales)


def condition(core_ref, *refs):
    grads_refs, column_refs, (out_ref, grads, weights) = refs[:ROWS_Y], refs[ROWS_Y:-3], refs[-3:]
    rows, columns = grads_refs[0].shape[0], column_refs[0].shape[1]
    for d, ref in enumerate(grads_refs):
        grads[d * rows : (d + 1) * rows, :] = ref[...]
    for core in range(CORES):

        @pl.when(core_ref[0] == core)
        def _():
            for i, ref in enumerate(column_refs):
                at = (i ^ core) * columns
                weights[:, at : at + columns] = ref[...]

    part = jnp.dot(grads[...], weights[...], preferred_element_type=jnp.float32)
    for chip in range(out_ref.shape[0]):
        out_ref[chip] = part.astype(out_ref.dtype)


def conditioned_for(core, chips, grads, columns):
    rows, width = len(grads) * grads[0].shape[0], grads[0].shape[1]
    out = len(columns) * columns[0].shape[1]
    return pl.pallas_call(
        condition,
        in_specs=[pl.BlockSpec(memory_space=pltpu.SMEM)]
        + [pl.BlockSpec(memory_space=pltpu.VMEM)] * (len(grads) + len(columns)),
        out_specs=pl.BlockSpec(memory_space=pltpu.VMEM),
        out_shape=jax.ShapeDtypeStruct((chips, rows, out), jnp.bfloat16),
        scratch_shapes=[pltpu.VMEM((rows, width), jnp.bfloat16), pltpu.VMEM((width, out), jnp.bfloat16)],
        compiler_params=pltpu.CompilerParams(vmem_limit_bytes=24 * MIB),
        cost_estimate=pl.CostEstimate(
            flops=2 * rows * width * out,
            bytes_accessed=2 * (rows * width + width * out + chips * rows * out),
            transcendentals=0,
        ),
    )(core, *grads, *columns)


def score(core_ref, parts_ref, mine_ref, theirs_ref, out_ref, queries):
    chip_rows, columns = parts_ref.shape[1], parts_ref.shape[2] // ROWS_X
    rows = chip_rows // ROWS_Y
    step, half = pl.program_id(0), pl.num_programs(0) // CORES

    @pl.when(step == 0)
    def _():
        for x in range(ROWS_X):
            for y in range(ROWS_Y):
                for k in range(ROWS_X):
                    at = ((x ^ k) * ROWS_Y + y) * columns
                    for d in range(ROWS_Y):
                        to = x * chip_rows + (y - d) % ROWS_Y * rows
                        queries[to : to + rows, at : at + columns] = parts_ref[
                            x * ROWS_Y + y, d * rows : (d + 1) * rows, k * columns : (k + 1) * columns
                        ]

    def times(store_ref):
        term = lax.dot_general(
            queries[...], store_ref[...], (((1,), (1,)), ((), ())),
            preferred_element_type=jnp.float32,
        ).astype(out_ref.dtype)
        tile = term.shape[0] // (PAIRS * NEAR)
        for pair in range(PAIRS):
            for near in range(NEAR):
                row = (pair * NEAR + near) * tile
                out_ref[near, pair * tile : (pair + 1) * tile, :] = term[row : row + tile, :]

    @pl.when(step < half)
    def _():
        times(mine_ref)

    @pl.when(step >= half)
    def _():
        times(theirs_ref)


def scores_of(core, parts, mine, theirs):
    chips, chip_rows, columns = parts.shape
    rows = ROWS_X * chip_rows
    examples, width = mine.shape
    tile = 256
    half = examples // tile
    whole = lambda n, core_ref: (0, 0, 0)
    return pl.pallas_call(
        score,
        grid_spec=pltpu.PrefetchScalarGridSpec(
            num_scalar_prefetch=1,
            grid=(CORES * half,),
            in_specs=[
                pl.BlockSpec((chips, chip_rows, columns), whole),
                pl.BlockSpec((tile, width), lambda n, core_ref: (jnp.minimum(n, half - 1), 0)),
                pl.BlockSpec((tile, width), lambda n, core_ref: (jnp.maximum(n - half, 0), 0)),
            ],
            out_specs=pl.BlockSpec(
                (NEAR, rows // NEAR, tile),
                lambda n, core_ref: (0, 0, (n + core_ref[0] * half) % (CORES * half)),
            ),
            scratch_shapes=[pltpu.VMEM((rows, width), jnp.bfloat16)],
        ),
        out_shape=jax.ShapeDtypeStruct((NEAR, rows // NEAR, CORES * examples), jnp.bfloat16),
        compiler_params=pltpu.CompilerParams(vmem_limit_bytes=32 * MIB),
        cost_estimate=pl.CostEstimate(
            flops=2 * rows * width * CORES * examples,
            bytes_accessed=2 * (rows * width + CORES * (width + rows) * examples),
            transcendentals=0,
        ),
    )(core, parts, mine, theirs)


def add(terms_ref, out_ref):
    examples = out_ref.shape[2]
    for c in range(CORES):
        columns = slice(c * examples, (c + 1) * examples)
        total = terms_ref[0, :, columns].astype(jnp.float32)
        for i in range(1, NEAR):
            total += terms_ref[i, :, columns].astype(jnp.float32)
        for p in range(out_ref.shape[0] // CORES):
            tile = out_ref.shape[1]
            out_ref[p * CORES + c] = total[p * tile : (p + 1) * tile].astype(out_ref.dtype)


def added(terms, tile, examples):
    steps = 4
    rows = terms.shape[1] // steps
    return pl.pallas_call(
        add,
        grid=(steps,),
        in_specs=[pl.BlockSpec((NEAR, rows, CORES * examples), lambda s: (0, s, 0))],
        out_specs=pl.BlockSpec((PAIRS * CORES // steps, tile, examples), lambda s: (s, 0, 0)),
        out_shape=jax.ShapeDtypeStruct((PAIRS * CORES, tile, examples), jnp.bfloat16),
        compiler_params=pltpu.CompilerParams(vmem_limit_bytes=16 * MIB),
        cost_estimate=pl.CostEstimate(
            flops=terms.size, bytes_accessed=3 * terms.size, transcendentals=0
        ),
    )(terms)


def shards(query_grads, precond, codes, scales):
    own_queries, width = query_grads.shape
    examples = codes.shape[0]
    ex_size, slots = lax.axis_size("ex"), lax.axis_size("dim")
    tile = own_queries * ex_size // slots // CORES
    chips = ROWS_X * ROWS_Y
    core = lax.axis_index("ex") % CORES
    core_swap = [(e, e ^ 1) for e in range(ex_size)]
    x_swap = [(e, e ^ (ROWS_Y * CORES)) for e in range(ex_size)]

    def y_shift(d):
        width_y = ROWS_Y * CORES
        return [(e, e // width_y * width_y + (e + d * CORES) % width_y) for e in range(ex_size)]

    same_core = [[chip * CORES + c for chip in range(chips)] for c in range(CORES)]
    near = [[pair * NEAR + i for i in range(NEAR)] for pair in range(PAIRS)]
    far = [
        [(chip * CORES + c) * slots + pair * NEAR + i for pair in range(PAIRS) for c in range(CORES)]
        for chip in range(chips)
        for i in range(NEAR)
    ]

    rows = query_grads.reshape(2, CORES, tile, width)
    kept = jnp.where(core == 0, rows[:, 0], rows[:, 1])
    swapped = lax.ppermute(jnp.where(core == 0, rows[:, 1], rows[:, 0]), "ex", core_swap)
    ours = jnp.concatenate(
        [jnp.where(core == 0, kept, swapped), jnp.where(core == 0, swapped, kept)], axis=0
    ).reshape(CORES * 2 * tile, width)
    above, below = (lax.ppermute(ours, "ex", y_shift(d)) for d in (1, ROWS_Y - 1))

    own = precond[0]
    across = lax.ppermute(own, "ex", x_swap)
    own_other = lax.ppermute(own, "ex", core_swap)
    across, own_other, above, below = lax.optimization_barrier((across, own_other, above, below))
    opposite = lax.ppermute(above, "ex", y_shift(1))
    across_other = lax.ppermute(across, "ex", core_swap)
    mine = dequantized(codes, scales)
    across_other, opposite, mine = lax.optimization_barrier((across_other, opposite, mine))

    parts = lax.all_to_all(
        conditioned_for(
            core.reshape(1), chips,
            [ours, above, opposite, below],
            [own, own_other, across, across_other],
        ),
        "ex", 0, 0, tiled=True, axis_index_groups=same_core,
    )

    theirs = lax.ppermute(mine, "ex", core_swap)

    terms = lax.all_to_all(
        scores_of(core.reshape(1), parts, mine, theirs),
        "dim", 0, 0, tiled=True, axis_index_groups=near,
    )
    sums = lax.all_to_all(
        added(terms, tile, examples), ("ex", "dim"), 0, 0, tiled=True, axis_index_groups=far
    )
    total = jnp.sum(sums.astype(jnp.float32).reshape(PAIRS, CORES * tile, examples), axis=0)
    return total * float(width * slots) ** (-0.5)


def solution(mesh):
    placed = (P("ex", "dim"), P("dim", None, "ex"), P("ex", "dim"), P("ex", "dim"))
    return jax.shard_map(
        shards, mesh=mesh, in_specs=placed, out_specs=P("dim", "ex"), check_vma=False
    )
```

```python
import functools

import jax
import jax.numpy as jnp
from jax import lax
from jax.experimental import pallas as pl
from jax.experimental.pallas import tpu as pltpu
from jax.sharding import PartitionSpec as P

CORES, ROWS_Y, ROWS_X = 2, 4, 2
PAIRS, SIDES = 8, 2
NEAR = 2 * SIDES
MIB = 1 << 20


def dequantize(codes_ref, scales_ref, out_ref):
    block = codes_ref.shape[1] // scales_ref.shape[1]
    for b in range(scales_ref.shape[1]):
        columns = slice(b * block, (b + 1) * block)
        entries = codes_ref[:, columns].astype(jnp.float32) * scales_ref[:, b : b + 1]
        out_ref[:, columns] = entries.astype(out_ref.dtype)


def dequantized(codes, scales):
    rows, width = codes.shape
    tile = 256
    return pl.pallas_call(
        dequantize,
        grid=(rows // tile,),
        in_specs=[
            pl.BlockSpec((tile, width), lambda r: (r, 0)),
            pl.BlockSpec((tile, scales.shape[1]), lambda r: (r, 0)),
        ],
        out_specs=pl.BlockSpec((tile, width), lambda r: (r, 0)),
        out_shape=jax.ShapeDtypeStruct(codes.shape, jnp.bfloat16),
        compiler_params=pltpu.CompilerParams(vmem_limit_bytes=56 * MIB),
        cost_estimate=pl.CostEstimate(
            flops=rows * width, bytes_accessed=4 * rows * width, transcendentals=0
        ),
    )(codes, scales)


def copy_halves(grads_ref, out_ref):
    tile = out_ref.shape[1] // 2
    for b in range(2):
        for core in range(CORES):
            row = (b * CORES + core) * tile
            entries = grads_ref[row : row + tile, :]
            for y in range(ROWS_Y):
                out_ref[y * CORES + core, b * tile : (b + 1) * tile, :] = entries


def spread(grads, tile):
    rows, width = grads.shape
    return pl.pallas_call(
        copy_halves,
        in_specs=[pl.BlockSpec(memory_space=pltpu.VMEM)],
        out_specs=pl.BlockSpec(memory_space=pltpu.VMEM),
        out_shape=jax.ShapeDtypeStruct((ROWS_Y * CORES, 2 * tile, width), grads.dtype),
        compiler_params=pltpu.CompilerParams(vmem_limit_bytes=8 * MIB),
        cost_estimate=pl.CostEstimate(
            flops=0, bytes_accessed=2 * (1 + ROWS_Y) * rows * width, transcendentals=0
        ),
    )(grads)


def condition(place_ref, *refs):
    grads_ref, column_refs, (part_ref, parts_ref, weights) = refs[0], refs[1:-3], refs[-3:]
    columns = column_refs[0].shape[1]
    for core in range(CORES):

        @pl.when(place_ref[0] == core)
        def _():
            for i, ref in enumerate(column_refs):
                at = (i ^ core) * columns
                weights[:, at : at + columns] = ref[...]

    part = jnp.dot(grads_ref[...], weights[...], preferred_element_type=jnp.float32)
    part_ref[...] = part.astype(part_ref.dtype)
    for y in range(ROWS_Y):
        parts_ref[y] = part.astype(part_ref.dtype)


def conditioned_for(place, grads, columns):
    rows, width = grads.shape
    out = len(columns) * columns[0].shape[1]
    return pl.pallas_call(
        condition,
        in_specs=[pl.BlockSpec(memory_space=pltpu.SMEM)]
        + [pl.BlockSpec(memory_space=pltpu.VMEM)] * (1 + len(columns)),
        out_specs=[pl.BlockSpec(memory_space=pltpu.VMEM)] * 2,
        out_shape=[
            jax.ShapeDtypeStruct((rows, out), jnp.bfloat16),
            jax.ShapeDtypeStruct((ROWS_Y, rows, out), jnp.bfloat16),
        ],
        scratch_shapes=[pltpu.VMEM((width, out), jnp.bfloat16)],
        compiler_params=pltpu.CompilerParams(vmem_limit_bytes=12 * MIB),
        cost_estimate=pl.CostEstimate(
            flops=2 * rows * width * out,
            bytes_accessed=2 * (rows * width + width * out + (1 + ROWS_Y) * rows * out),
            transcendentals=0,
        ),
    )(place, grads, *columns)


def score(far, place_ref, *refs):
    part_refs, (mine_ref, theirs_ref, out_ref, queries) = refs[:ROWS_Y], refs[-4:]
    block_rows, columns = part_refs[0].shape[0], part_refs[0].shape[1] // ROWS_X
    rows = block_rows // ROWS_Y
    step, half = pl.program_id(0), pl.num_programs(0) // CORES

    @pl.when(step == 0)
    def _():
        x = lax.rem(place_ref[2] + far, ROWS_X)
        for i, ref in enumerate(part_refs):
            y = lax.rem(place_ref[1] + ROWS_Y - i, ROWS_Y) if far else i
            for k in range(ROWS_X):
                at = (lax.rem(x + k, ROWS_X) * ROWS_Y + y) * columns
                queries[:, pl.ds(pl.multiple_of(at, columns), columns)] = ref[
                    :, k * columns : (k + 1) * columns
                ]

    def times(store_ref):
        term = lax.dot_general(
            queries[...], store_ref[...], (((1,), (1,)), ((), ())),
            preferred_element_type=jnp.float32,
        ).astype(out_ref.dtype)
        tile = rows // NEAR
        for y in range(ROWS_Y):
            for near in range(NEAR):
                row = y * rows + near * tile
                out_ref[near, y * tile : (y + 1) * tile, :] = term[row : row + tile, :]

    @pl.when(step < half)
    def _():
        times(mine_ref)

    @pl.when(step >= half)
    def _():
        times(theirs_ref)


def scores_of(far, place, parts, mine, theirs, before=None):
    columns = parts[0].shape[-1]
    rows = parts[0].shape[-2]
    examples, width = mine.shape
    tile = 512
    half = examples // tile
    if far:
        part_specs = [pl.BlockSpec((rows, columns), lambda n, place_ref: (0, 0))] * ROWS_Y
    else:
        part_specs = [
            pl.BlockSpec((pl.squeezed, rows, columns), lambda n, place_ref, y=y: (y, 0, 0))
            for y in range(ROWS_Y)
        ]
    body = functools.partial(score, far)
    if before is not None:
        body = lambda place_ref, before_ref, *refs: score(far, place_ref, *refs)
    return pl.pallas_call(
        body,
        grid_spec=pltpu.PrefetchScalarGridSpec(
            num_scalar_prefetch=1,
            grid=(CORES * half,),
            in_specs=([] if before is None else [pl.BlockSpec(memory_space=pl.ANY)])
            + part_specs
            + [
                pl.BlockSpec((tile, width), lambda n, place_ref: (jnp.minimum(n, half - 1), 0)),
                pl.BlockSpec((tile, width), lambda n, place_ref: (jnp.maximum(n - half, 0), 0)),
            ],
            out_specs=pl.BlockSpec(
                (NEAR, rows // NEAR, tile),
                lambda n, place_ref: (
                    0,
                    lax.rem(place_ref[2] + far, ROWS_X),
                    lax.rem(n + place_ref[0] * half, CORES * half),
                ),
            ),
            scratch_shapes=[pltpu.VMEM((rows, width), jnp.bfloat16)],
        ),
        out_shape=jax.ShapeDtypeStruct((NEAR, ROWS_X * rows // NEAR, CORES * examples), jnp.bfloat16),
        input_output_aliases={} if before is None else {1: 0},
        compiler_params=pltpu.CompilerParams(vmem_limit_bytes=50 * MIB),
        cost_estimate=pl.CostEstimate(
            flops=2 * rows * width * CORES * examples,
            bytes_accessed=2 * (rows * width + CORES * (width + rows) * examples),
            transcendentals=0,
        ),
    )(place, *([] if before is None else [before]), *parts, mine, theirs)


def add(terms_ref, out_ref):
    examples = out_ref.shape[2]
    for c in range(CORES):
        columns = slice(c * examples, (c + 1) * examples)
        total = terms_ref[0, :, columns].astype(jnp.float32)
        for i in range(1, NEAR):
            total += terms_ref[i, :, columns].astype(jnp.float32)
        for p in range(out_ref.shape[0] // CORES):
            tile = out_ref.shape[1]
            out_ref[p * CORES + c] = total[p * tile : (p + 1) * tile].astype(out_ref.dtype)


def added(terms, tile, examples):
    steps = 4
    rows = terms.shape[1] // steps
    return pl.pallas_call(
        add,
        grid=(steps,),
        in_specs=[pl.BlockSpec((NEAR, rows, CORES * examples), lambda s: (0, s, 0))],
        out_specs=pl.BlockSpec((PAIRS * CORES // steps, tile, examples), lambda s: (s, 0, 0)),
        out_shape=jax.ShapeDtypeStruct((PAIRS * CORES, tile, examples), jnp.bfloat16),
        compiler_params=pltpu.CompilerParams(vmem_limit_bytes=8 * MIB),
        cost_estimate=pl.CostEstimate(
            flops=terms.size, bytes_accessed=3 * terms.size, transcendentals=0
        ),
    )(terms)


def shards(query_grads, precond, codes, scales):
    own_queries, width = query_grads.shape
    examples = codes.shape[0]
    ex_size, slots = lax.axis_size("ex"), lax.axis_size("dim")
    tile = own_queries * ex_size // slots // CORES
    chips = ROWS_X * ROWS_Y
    position = lax.axis_index("ex")
    place = jnp.stack([position % CORES, position // CORES % ROWS_Y, position // (CORES * ROWS_Y)])
    spots = [(x, y, c) for x in range(ROWS_X) for y in range(ROWS_Y) for c in range(CORES)]

    def shift(x_by, y_by, core_by):
        return [
            (e, ((x + x_by) % ROWS_X * ROWS_Y + (y + y_by) % ROWS_Y) * CORES + (c + core_by) % CORES)
            for e, (x, y, c) in enumerate(spots)
        ]

    chip_group = ROWS_Y * CORES
    beside = [list(range(x * chip_group, (x + 1) * chip_group)) for x in range(ROWS_X)]
    along_y = [
        [(x * ROWS_Y + y) * CORES + c for y in range(ROWS_Y)] for x in range(ROWS_X) for c in range(CORES)
    ]
    near = [[pair * NEAR + i for i in range(NEAR)] for pair in range(PAIRS)]
    far = [
        [(chip * CORES + c) * slots + pair * NEAR + i for pair in range(PAIRS) for c in range(CORES)]
        for chip in range(chips)
        for i in range(NEAR)
    ]

    own = precond[0]
    columns = [own] + [
        lax.ppermute(own, "ex", shift(x, 0, c)) for x, c in ((0, 1), (1, 0), (1, 1))
    ]

    grads = lax.all_to_all(
        spread(query_grads, tile),
        "ex", 0, 0, tiled=True, axis_index_groups=beside,
    ).reshape(ROWS_Y * CORES * 2 * tile, width)

    mine = dequantized(codes, scales)
    grads, mine, *columns = lax.optimization_barrier((grads, mine, *columns))
    part, copies = conditioned_for(place, grads, columns)
    theirs = lax.ppermute(mine, "ex", shift(0, 0, 1))

    parts = lax.all_to_all(copies, "ex", 0, 0, tiled=True, axis_index_groups=along_y)
    others = [lax.ppermute(part, "ex", shift(1, y, 0)) for y in range(ROWS_Y)]

    terms = scores_of(0, place, [parts] * ROWS_Y, mine, theirs)
    terms = scores_of(1, place, others, mine, theirs, terms)
    terms = lax.all_to_all(terms, "dim", 0, 0, tiled=True, axis_index_groups=near)
    sums = lax.all_to_all(
        added(terms, tile, examples), ("ex", "dim"), 0, 0, tiled=True, axis_index_groups=far
    )
    total = jnp.sum(sums.astype(jnp.float32).reshape(PAIRS, CORES * tile, examples), axis=0)
    return total * float(width * slots) ** (-0.5)


def solution(mesh):
    placed = (P("ex", "dim"), P("dim", None, "ex"), P("ex", "dim"), P("ex", "dim"))
    return jax.shard_map(
        shards, mesh=mesh, in_specs=placed, out_specs=P("dim", "ex"), check_vma=False
    )
```

```python
import jax
import jax.numpy as jnp
from jax import lax
from jax.experimental import pallas as pl
from jax.experimental.pallas import tpu as pltpu
from jax.sharding import PartitionSpec as P

CORES, ROWS_Y, ROWS_X = 2, 4, 2
PAIRS, SIDES = 8, 2
NEAR = 2 * SIDES
MIB = 1 << 20


def dequantize(codes_ref, scales_ref, out_ref):
    block = codes_ref.shape[1] // scales_ref.shape[1]
    for b in range(scales_ref.shape[1]):
        columns = slice(b * block, (b + 1) * block)
        entries = codes_ref[:, columns].astype(jnp.float32) * scales_ref[:, b : b + 1]
        out_ref[:, columns] = entries.astype(out_ref.dtype)


def dequantized(codes, scales):
    rows, width = codes.shape
    tile = 256
    return pl.pallas_call(
        dequantize,
        grid=(rows // tile,),
        in_specs=[
            pl.BlockSpec((tile, width), lambda r: (r, 0)),
            pl.BlockSpec((tile, scales.shape[1]), lambda r: (r, 0)),
        ],
        out_specs=pl.BlockSpec((tile, width), lambda r: (r, 0)),
        out_shape=jax.ShapeDtypeStruct(codes.shape, jnp.bfloat16),
        compiler_params=pltpu.CompilerParams(vmem_limit_bytes=56 * MIB),
        cost_estimate=pl.CostEstimate(
            flops=rows * width, bytes_accessed=4 * rows * width, transcendentals=0
        ),
    )(codes, scales)


def copy_halves(grads_ref, out_ref):
    tile = out_ref.shape[1] // 2
    for b in range(2):
        for core in range(CORES):
            row = (b * CORES + core) * tile
            entries = grads_ref[row : row + tile, :]
            for y in range(ROWS_Y):
                out_ref[y * CORES + core, b * tile : (b + 1) * tile, :] = entries


def spread(grads, tile):
    rows, width = grads.shape
    return pl.pallas_call(
        copy_halves,
        in_specs=[pl.BlockSpec(memory_space=pltpu.VMEM)],
        out_specs=pl.BlockSpec(memory_space=pltpu.VMEM),
        out_shape=jax.ShapeDtypeStruct((ROWS_Y * CORES, 2 * tile, width), grads.dtype),
        compiler_params=pltpu.CompilerParams(vmem_limit_bytes=8 * MIB),
        cost_estimate=pl.CostEstimate(
            flops=0, bytes_accessed=2 * (1 + ROWS_Y) * rows * width, transcendentals=0
        ),
    )(grads)


def condition(place_ref, *refs):
    grads_ref, column_refs, (parts_ref, weights) = refs[0], refs[1:-2], refs[-2:]
    columns = column_refs[0].shape[1]
    for core in range(CORES):

        @pl.when(place_ref[0] == core)
        def _():
            for i, ref in enumerate(column_refs):
                at = (i ^ core) * columns
                weights[:, at : at + columns] = ref[...]

    part = jnp.dot(grads_ref[...], weights[...], preferred_element_type=jnp.float32)
    for chip in range(parts_ref.shape[0]):
        parts_ref[chip] = part.astype(parts_ref.dtype)


def conditioned_for(place, chips, grads, columns):
    rows, width = grads.shape
    out = len(columns) * columns[0].shape[1]
    return pl.pallas_call(
        condition,
        in_specs=[pl.BlockSpec(memory_space=pltpu.SMEM)]
        + [pl.BlockSpec(memory_space=pltpu.VMEM)] * (1 + len(columns)),
        out_specs=pl.BlockSpec(memory_space=pltpu.VMEM),
        out_shape=jax.ShapeDtypeStruct((chips, rows, out), jnp.bfloat16),
        scratch_shapes=[pltpu.VMEM((width, out), jnp.bfloat16)],
        compiler_params=pltpu.CompilerParams(vmem_limit_bytes=16 * MIB),
        cost_estimate=pl.CostEstimate(
            flops=2 * rows * width * out,
            bytes_accessed=2 * (rows * width + width * out + chips * rows * out),
            transcendentals=0,
        ),
    )(place, grads, *columns)


def score(place_ref, parts_ref, store_ref, *refs):
    out_refs, queries = refs[:NEAR], refs[NEAR]
    block_rows, columns = parts_ref.shape[1], parts_ref.shape[2] // ROWS_X
    rows = block_rows // ROWS_Y
    tile = rows // NEAR

    @pl.when(pl.program_id(0) == 0)
    def _():
        for x in range(ROWS_X):
            for pair in range(ROWS_Y):
                for near in range(NEAR):
                    to = (near ^ place_ref[1]) * (PAIRS * tile) + (x * ROWS_Y + pair) * tile
                    to = pl.multiple_of(to, tile)
                    row = pair * rows + near * tile
                    for y in range(ROWS_Y):
                        for k in range(ROWS_X):
                            at = ((x ^ k) * ROWS_Y + y) * columns
                            queries[pl.ds(to, tile), at : at + columns] = parts_ref[
                                x * ROWS_Y + y, row : row + tile, k * columns : (k + 1) * columns
                            ]

    term = lax.dot_general(
        queries[...], store_ref[...], (((1,), (1,)), ((), ())),
        preferred_element_type=jnp.float32,
    )
    for k, ref in enumerate(out_refs):
        ref[...] = term[k * PAIRS * tile : (k + 1) * PAIRS * tile].astype(ref.dtype)


def scores_of(place, parts, store):
    chips, block_rows, columns = parts.shape
    rows = ROWS_X * block_rows
    examples, width = store.shape
    tile = 256
    return pl.pallas_call(
        score,
        grid_spec=pltpu.PrefetchScalarGridSpec(
            num_scalar_prefetch=1,
            grid=(examples // tile,),
            in_specs=[
                pl.BlockSpec((chips, block_rows, columns), lambda n, place_ref: (0, 0, 0)),
                pl.BlockSpec((tile, width), lambda n, place_ref: (n, 0)),
            ],
            out_specs=[pl.BlockSpec((rows // NEAR, tile), lambda n, place_ref: (0, n))] * NEAR,
            scratch_shapes=[pltpu.VMEM((rows, width), jnp.bfloat16)],
        ),
        out_shape=[jax.ShapeDtypeStruct((rows // NEAR, examples), jnp.bfloat16)] * NEAR,
        compiler_params=pltpu.CompilerParams(vmem_limit_bytes=32 * MIB),
        cost_estimate=pl.CostEstimate(
            flops=2 * rows * width * examples,
            bytes_accessed=2 * (rows * width + (width + rows) * examples),
            transcendentals=0,
        ),
    )(place, parts, store)


def add(place_ref, *refs):
    out_ref = refs[-1]
    tile = out_ref.shape[1]
    for i in range(CORES):
        total = refs[i * NEAR][...].astype(jnp.float32)
        for ref in refs[i * NEAR + 1 : (i + 1) * NEAR]:
            total += ref[...].astype(jnp.float32)
        for p in range(out_ref.shape[0] // CORES):
            at = p * CORES + (place_ref[0] ^ i)
            out_ref[at] = total[p * tile : (p + 1) * tile].astype(out_ref.dtype)


def added(place, tile, terms):
    steps = 4
    rows, examples = terms[0].shape
    return pl.pallas_call(
        add,
        grid_spec=pltpu.PrefetchScalarGridSpec(
            num_scalar_prefetch=1,
            grid=(steps,),
            in_specs=[pl.BlockSpec((rows // steps, examples), lambda s, place_ref: (s, 0))] * len(terms),
            out_specs=pl.BlockSpec(
                (PAIRS * CORES // steps, tile, examples), lambda s, place_ref: (s, 0, 0)
            ),
        ),
        out_shape=jax.ShapeDtypeStruct((PAIRS * CORES, tile, examples), jnp.bfloat16),
        compiler_params=pltpu.CompilerParams(vmem_limit_bytes=16 * MIB),
        cost_estimate=pl.CostEstimate(
            flops=len(terms) * rows * examples,
            bytes_accessed=3 * len(terms) * rows * examples,
            transcendentals=0,
        ),
    )(place, *terms)


def shards(query_grads, precond, codes, scales):
    own_queries, width = query_grads.shape
    examples = codes.shape[0]
    ex_size, slots = lax.axis_size("ex"), lax.axis_size("dim")
    tile = own_queries * ex_size // slots // CORES
    chips = ROWS_X * ROWS_Y
    position = lax.axis_index("ex")
    near_here = lax.axis_index("dim") % NEAR
    place = jnp.stack([position % CORES, near_here])
    spots = [(x, y, c) for x in range(ROWS_X) for y in range(ROWS_Y) for c in range(CORES)]

    def shift(x_by, y_by, core_by):
        return [
            (e, ((x + x_by) % ROWS_X * ROWS_Y + (y + y_by) % ROWS_Y) * CORES + (c + core_by) % CORES)
            for e, (x, y, c) in enumerate(spots)
        ]

    chip_group = ROWS_Y * CORES
    beside = [list(range(x * chip_group, (x + 1) * chip_group)) for x in range(ROWS_X)]
    same_core = [[chip * CORES + c for chip in range(chips)] for c in range(CORES)]
    far = [
        [(chip * CORES + c) * slots + pair * NEAR + i for pair in range(PAIRS) for c in range(CORES)]
        for chip in range(chips)
        for i in range(NEAR)
    ]

    own = precond[0]
    own_other = lax.ppermute(own, "ex", shift(0, 0, 1))
    across = lax.ppermute(own, "ex", shift(1, 0, 0))
    across_other = lax.ppermute(across, "ex", shift(0, 0, 1))

    grads = lax.all_to_all(
        spread(query_grads, tile), "ex", 0, 0, tiled=True, axis_index_groups=beside
    ).reshape(ROWS_Y * CORES * 2 * tile, width)

    mine = dequantized(codes, scales)
    grads, mine, own_other, across, across_other = lax.optimization_barrier(
        (grads, mine, own_other, across, across_other)
    )
    copies = conditioned_for(place, chips, grads, [own, own_other, across, across_other])
    mine, copies = lax.optimization_barrier((mine, copies))
    theirs = lax.ppermute(mine, "ex", shift(0, 0, 1))
    parts = lax.all_to_all(copies, "ex", 0, 0, tiled=True, axis_index_groups=same_core)

    terms = []
    for store in (mine, theirs):
        here, *away = scores_of(place, parts, store)
        terms += [here] + [
            lax.ppermute(term, "dim", [(d, d ^ k) for d in range(slots)])
            for k, term in enumerate(away, 1)
        ]
    sums = lax.all_to_all(
        added(place, tile, terms), ("ex", "dim"), 0, 0, tiled=True, axis_index_groups=far
    )
    total = jnp.sum(sums.astype(jnp.float32).reshape(PAIRS, CORES * tile, examples), axis=0)
    return total * float(width * slots) ** (-0.5)


def solution(mesh):
    placed = (P("ex", "dim"), P("dim", None, "ex"), P("ex", "dim"), P("ex", "dim"))
    return jax.shard_map(
        shards, mesh=mesh, in_specs=placed, out_specs=P("dim", "ex"), check_vma=False
    )
```

```python
import functools

import jax
import jax.numpy as jnp
from jax import lax
from jax.experimental import pallas as pl
from jax.experimental.pallas import tpu as pltpu
from jax.sharding import PartitionSpec as P

CORES, ROWS_Y, ROWS_X = 2, 4, 2
PAIRS, SIDES = 8, 2
NEAR = 2 * SIDES
MIB = 1 << 20


def dequantize(codes_ref, scales_ref, out_ref):
    block = codes_ref.shape[1] // scales_ref.shape[1]
    for b in range(scales_ref.shape[1]):
        columns = slice(b * block, (b + 1) * block)
        entries = codes_ref[:, columns].astype(jnp.float32) * scales_ref[:, b : b + 1]
        out_ref[:, columns] = entries.astype(out_ref.dtype)


def dequantized(codes, scales):
    rows, width = codes.shape
    tile = 256
    return pl.pallas_call(
        dequantize,
        grid=(rows // tile,),
        in_specs=[
            pl.BlockSpec((tile, width), lambda r: (r, 0)),
            pl.BlockSpec((tile, scales.shape[1]), lambda r: (r, 0)),
        ],
        out_specs=pl.BlockSpec((tile, width), lambda r: (r, 0)),
        out_shape=jax.ShapeDtypeStruct(codes.shape, jnp.bfloat16),
        compiler_params=pltpu.CompilerParams(vmem_limit_bytes=56 * MIB),
        cost_estimate=pl.CostEstimate(
            flops=rows * width, bytes_accessed=4 * rows * width, transcendentals=0
        ),
    )(codes, scales)


def copy_halves(grads_ref, out_ref):
    tile = out_ref.shape[1] // 2
    for b in range(2):
        for core in range(CORES):
            row = (b * CORES + core) * tile
            entries = grads_ref[row : row + tile, :]
            for y in range(ROWS_Y):
                out_ref[y * CORES + core, b * tile : (b + 1) * tile, :] = entries


def spread(grads, tile):
    rows, width = grads.shape
    return pl.pallas_call(
        copy_halves,
        in_specs=[pl.BlockSpec(memory_space=pltpu.VMEM)],
        out_specs=pl.BlockSpec(memory_space=pltpu.VMEM),
        out_shape=jax.ShapeDtypeStruct((ROWS_Y * CORES, 2 * tile, width), grads.dtype),
        compiler_params=pltpu.CompilerParams(vmem_limit_bytes=8 * MIB),
        cost_estimate=pl.CostEstimate(
            flops=0, bytes_accessed=2 * (1 + ROWS_Y) * rows * width, transcendentals=0
        ),
    )(grads)


def condition(place_ref, *refs):
    grads_ref, column_refs, (parts_ref, weights) = refs[0], refs[1:-2], refs[-2:]
    columns = column_refs[0].shape[1]
    for core in range(CORES):

        @pl.when(place_ref[0] == core)
        def _():
            for i, ref in enumerate(column_refs):
                at = (i ^ core) * columns
                weights[:, at : at + columns] = ref[...]

    part = jnp.dot(grads_ref[...], weights[...], preferred_element_type=jnp.float32)
    for chip in range(parts_ref.shape[0]):
        parts_ref[chip] = part.astype(parts_ref.dtype)


def conditioned_for(place, chips, grads, columns):
    rows, width = grads.shape
    out = len(columns) * columns[0].shape[1]
    return pl.pallas_call(
        condition,
        in_specs=[pl.BlockSpec(memory_space=pltpu.SMEM)]
        + [pl.BlockSpec(memory_space=pltpu.VMEM)] * (1 + len(columns)),
        out_specs=pl.BlockSpec(memory_space=pltpu.VMEM),
        out_shape=jax.ShapeDtypeStruct((chips, rows, out), jnp.bfloat16),
        scratch_shapes=[pltpu.VMEM((width, out), jnp.bfloat16)],
        compiler_params=pltpu.CompilerParams(vmem_limit_bytes=16 * MIB),
        cost_estimate=pl.CostEstimate(
            flops=2 * rows * width * out,
            bytes_accessed=2 * (rows * width + width * out + chips * rows * out),
            transcendentals=0,
        ),
    )(place, grads, *columns)


def score(apart, place_ref, parts_ref, store_ref, *refs):
    out_refs, queries = refs[:-1], refs[-1]
    block_rows, columns = parts_ref.shape[1], parts_ref.shape[2] // ROWS_X
    rows = block_rows // ROWS_Y
    tile = rows // NEAR

    @pl.when(pl.program_id(0) == 0)
    def _():
        for x in range(ROWS_X):
            for pair in range(ROWS_Y):
                for near in range(NEAR):
                    to = (x * ROWS_Y + pair) * tile
                    if apart:
                        to = pl.multiple_of((near ^ place_ref[1]) * (PAIRS * tile) + to, tile)
                    else:
                        to += near * PAIRS * tile
                    row = pair * rows + near * tile
                    for y in range(ROWS_Y):
                        for k in range(ROWS_X):
                            at = ((x ^ k) * ROWS_Y + y) * columns
                            queries[pl.ds(to, tile), at : at + columns] = parts_ref[
                                x * ROWS_Y + y, row : row + tile, k * columns : (k + 1) * columns
                            ]

    term = lax.dot_general(
        queries[...], store_ref[...], (((1,), (1,)), ((), ())),
        preferred_element_type=jnp.float32,
    )
    for k in range(NEAR):
        entries = term[k * PAIRS * tile : (k + 1) * PAIRS * tile].astype(out_refs[0].dtype)
        if apart:
            out_refs[k][...] = entries
        else:
            out_refs[0][k] = entries


def scores_of(apart, place, parts, store):
    chips, block_rows, columns = parts.shape
    rows = ROWS_X * block_rows
    examples, width = store.shape
    tile = 256
    if apart:
        block, index, shape, count = (rows // NEAR, tile), lambda n, place_ref: (0, n), (rows // NEAR, examples), NEAR
    else:
        block, index = (NEAR, rows // NEAR, tile), lambda n, place_ref: (0, 0, n)
        shape, count = (NEAR, rows // NEAR, examples), 1
    return pl.pallas_call(
        functools.partial(score, apart),
        grid_spec=pltpu.PrefetchScalarGridSpec(
            num_scalar_prefetch=1,
            grid=(examples // tile,),
            in_specs=[
                pl.BlockSpec((chips, block_rows, columns), lambda n, place_ref: (0, 0, 0)),
                pl.BlockSpec((tile, width), lambda n, place_ref: (n, 0)),
            ],
            out_specs=[pl.BlockSpec(block, index)] * count,
            scratch_shapes=[pltpu.VMEM((rows, width), jnp.bfloat16)],
        ),
        out_shape=[jax.ShapeDtypeStruct(shape, jnp.bfloat16) if apart else pltpu.HBM(shape, jnp.bfloat16)] * count,
        compiler_params=pltpu.CompilerParams(vmem_limit_bytes=50 * MIB),
        cost_estimate=pl.CostEstimate(
            flops=2 * rows * width * examples,
            bytes_accessed=2 * (rows * width + (width + rows) * examples),
            transcendentals=0,
        ),
    )(place, parts, store)


def add(place_ref, gathered_ref, *refs):
    other_refs, out_ref = refs[:-1], refs[-1]
    tile = out_ref.shape[1]
    sums = gathered_ref[0].astype(jnp.float32), other_refs[0][...].astype(jnp.float32)
    for k in range(1, NEAR):
        sums = (
            sums[0] + gathered_ref[k].astype(jnp.float32),
            sums[1] + other_refs[k][...].astype(jnp.float32),
        )
    for i, total in enumerate(sums):
        for p in range(out_ref.shape[0] // CORES):
            at = p * CORES + (place_ref[0] ^ i)
            out_ref[at] = total[p * tile : (p + 1) * tile].astype(out_ref.dtype)


def added(place, tile, gathered, others):
    steps = 4
    rows, examples = others[0].shape
    return pl.pallas_call(
        add,
        grid_spec=pltpu.PrefetchScalarGridSpec(
            num_scalar_prefetch=1,
            grid=(steps,),
            in_specs=[pl.BlockSpec((NEAR, rows // steps, examples), lambda s, place_ref: (0, s, 0))]
            + [pl.BlockSpec((rows // steps, examples), lambda s, place_ref: (s, 0))] * NEAR,
            out_specs=pl.BlockSpec(
                (PAIRS * CORES // steps, tile, examples), lambda s, place_ref: (s, 0, 0)
            ),
        ),
        out_shape=jax.ShapeDtypeStruct((PAIRS * CORES, tile, examples), jnp.bfloat16),
        compiler_params=pltpu.CompilerParams(vmem_limit_bytes=16 * MIB),
        cost_estimate=pl.CostEstimate(
            flops=2 * NEAR * rows * examples,
            bytes_accessed=6 * NEAR * rows * examples,
            transcendentals=0,
        ),
    )(place, gathered, *others)


def shards(query_grads, precond, codes, scales):
    own_queries, width = query_grads.shape
    examples = codes.shape[0]
    ex_size, slots = lax.axis_size("ex"), lax.axis_size("dim")
    tile = own_queries * ex_size // slots // CORES
    chips = ROWS_X * ROWS_Y
    position = lax.axis_index("ex")
    near_here = lax.axis_index("dim") % NEAR
    place = jnp.stack([position % CORES, near_here])
    spots = [(x, y, c) for x in range(ROWS_X) for y in range(ROWS_Y) for c in range(CORES)]

    def shift(x_by, y_by, core_by):
        return [
            (e, ((x + x_by) % ROWS_X * ROWS_Y + (y + y_by) % ROWS_Y) * CORES + (c + core_by) % CORES)
            for e, (x, y, c) in enumerate(spots)
        ]

    chip_group = ROWS_Y * CORES
    beside = [list(range(x * chip_group, (x + 1) * chip_group)) for x in range(ROWS_X)]
    same_core = [[chip * CORES + c for chip in range(chips)] for c in range(CORES)]
    near = [[pair * NEAR + i for i in range(NEAR)] for pair in range(PAIRS)]
    far = [
        [(chip * CORES + c) * slots + pair * NEAR + i for pair in range(PAIRS) for c in range(CORES)]
        for chip in range(chips)
        for i in range(NEAR)
    ]

    own, halves = precond[0], spread(query_grads, tile)
    own_other = lax.ppermute(own, "ex", shift(0, 0, 1))
    across = lax.ppermute(own, "ex", shift(1, 0, 0))
    across_other = lax.ppermute(across, "ex", shift(0, 0, 1))

    grads = lax.all_to_all(
        halves, "ex", 0, 0, tiled=True, axis_index_groups=beside
    ).reshape(ROWS_Y * CORES * 2 * tile, width)

    mine = dequantized(codes, scales)
    grads, mine, own_other, across, across_other = lax.optimization_barrier(
        (grads, mine, own_other, across, across_other)
    )
    copies = conditioned_for(place, chips, grads, [own, own_other, across, across_other])
    mine, copies = lax.optimization_barrier((mine, copies))
    theirs = lax.ppermute(mine, "ex", shift(0, 0, 1))
    parts = lax.all_to_all(copies, "ex", 0, 0, tiled=True, axis_index_groups=same_core)

    (terms,) = scores_of(False, place, parts, mine)
    gathered = lax.all_to_all(terms, "dim", 0, 0, tiled=True, axis_index_groups=near)
    here, *away = scores_of(True, place, parts, theirs)
    others = [here] + [
        lax.ppermute(term, "dim", [(d, d ^ k) for d in range(slots)]) for k, term in enumerate(away, 1)
    ]
    sums = lax.all_to_all(
        added(place, tile, gathered, others), ("ex", "dim"), 0, 0, tiled=True, axis_index_groups=far
    )
    total = jnp.sum(sums.astype(jnp.float32).reshape(PAIRS, CORES * tile, examples), axis=0)
    return total * float(width * slots) ** (-0.5)


def solution(mesh):
    placed = (P("ex", "dim"), P("dim", None, "ex"), P("ex", "dim"), P("ex", "dim"))
    return jax.shard_map(
        shards, mesh=mesh, in_specs=placed, out_specs=P("dim", "ex"), check_vma=False
    )
```

```python
import functools

import jax
import jax.numpy as jnp
from jax import lax
from jax.experimental import pallas as pl
from jax.experimental.pallas import tpu as pltpu
from jax.sharding import PartitionSpec as P

CORES, ROWS_Y, ROWS_X = 2, 4, 2
PAIRS, SIDES = 8, 2
NEAR = 2 * SIDES
MIB = 1 << 20


def dequantize(codes_ref, scales_ref, out_ref):
    block = codes_ref.shape[1] // scales_ref.shape[1]
    for b in range(scales_ref.shape[1]):
        columns = slice(b * block, (b + 1) * block)
        entries = codes_ref[:, columns].astype(jnp.float32) * scales_ref[:, b : b + 1]
        out_ref[:, columns] = entries.astype(out_ref.dtype)


def dequantized(codes, scales):
    rows, width = codes.shape
    tile = 256
    return pl.pallas_call(
        dequantize,
        grid=(rows // tile,),
        in_specs=[
            pl.BlockSpec((tile, width), lambda r: (r, 0)),
            pl.BlockSpec((tile, scales.shape[1]), lambda r: (r, 0)),
        ],
        out_specs=pl.BlockSpec((tile, width), lambda r: (r, 0)),
        out_shape=jax.ShapeDtypeStruct(codes.shape, jnp.bfloat16),
        compiler_params=pltpu.CompilerParams(vmem_limit_bytes=56 * MIB),
        cost_estimate=pl.CostEstimate(
            flops=rows * width, bytes_accessed=4 * rows * width, transcendentals=0
        ),
    )(codes, scales)


def copy_all(copies):
    for copy in copies:
        copy.start()
    for copy in copies:
        copy.wait()


def copy_halves(grads_ref, out_ref, sems):
    tile = out_ref.shape[1] // 2
    copies = []
    for y in range(ROWS_Y):
        for core in range(CORES):
            for b in range(2):
                copies.append(
                    pltpu.make_async_copy(
                        grads_ref.at[pl.ds((b * CORES + core) * tile, tile)],
                        out_ref.at[y * CORES + core, pl.ds(b * tile, tile)],
                        sems.at[len(copies)],
                    )
                )
    copy_all(copies)


def spread(grads, tile):
    rows, width = grads.shape
    return pl.pallas_call(
        copy_halves,
        in_specs=[pl.BlockSpec(memory_space=pltpu.HBM)],
        out_specs=pl.BlockSpec(memory_space=pltpu.HBM),
        out_shape=pltpu.HBM((ROWS_Y * CORES, 2 * tile, width), grads.dtype),
        scratch_shapes=[pltpu.SemaphoreType.DMA((ROWS_Y * CORES * 2,))],
        compiler_params=pltpu.CompilerParams(vmem_limit_bytes=60 * MIB),
        cost_estimate=pl.CostEstimate(
            flops=0, bytes_accessed=2 * (1 + ROWS_Y) * rows * width, transcendentals=0
        ),
    )(grads)


def condition(place_ref, *refs):
    grads_ref, column_refs, (parts_ref, weights, block, sems) = refs[0], refs[1:-4], refs[-4:]
    columns = column_refs[0].shape[1]
    for core in range(CORES):

        @pl.when(place_ref[0] == core)
        def _():
            for i, ref in enumerate(column_refs):
                at = (i ^ core) * columns
                weights[:, at : at + columns] = ref[...]

    part = jnp.dot(grads_ref[...], weights[...], preferred_element_type=jnp.float32)
    block[...] = part.astype(block.dtype)
    copy_all(
        [
            pltpu.make_async_copy(block, parts_ref.at[chip], sems.at[chip])
            for chip in range(parts_ref.shape[0])
        ]
    )


def conditioned_for(place, chips, grads, columns):
    rows, width = grads.shape
    out = len(columns) * columns[0].shape[1]
    return pl.pallas_call(
        condition,
        in_specs=[pl.BlockSpec(memory_space=pltpu.SMEM)]
        + [pl.BlockSpec(memory_space=pltpu.VMEM)] * (1 + len(columns)),
        out_specs=pl.BlockSpec(memory_space=pltpu.HBM),
        out_shape=pltpu.HBM((chips, rows, out), jnp.bfloat16),
        scratch_shapes=[
            pltpu.VMEM((width, out), jnp.bfloat16),
            pltpu.VMEM((rows, out), jnp.bfloat16),
            pltpu.SemaphoreType.DMA((chips,)),
        ],
        compiler_params=pltpu.CompilerParams(vmem_limit_bytes=16 * MIB),
        cost_estimate=pl.CostEstimate(
            flops=2 * rows * width * out,
            bytes_accessed=2 * (rows * width + width * out + chips * rows * out),
            transcendentals=0,
        ),
    )(place, grads, *columns)


def score(apart, place_ref, parts_ref, store_ref, *refs):
    out_refs, (queries, held, ready, terms, sent) = refs[:-5], refs[-5:]
    block_rows, columns = parts_ref.shape[1], parts_ref.shape[2] // ROWS_X
    rows = block_rows // ROWS_Y
    tile = rows // NEAR
    steps = ready.shape[0]
    examples = held.shape[0] // steps
    copies = [
        pltpu.make_async_copy(
            store_ref.at[pl.ds(n * examples, examples)], held.at[pl.ds(n * examples, examples)], ready.at[n]
        )
        for n in range(steps)
    ]
    for copy in copies:
        copy.start()

    for x in range(ROWS_X):
        for pair in range(ROWS_Y):
            for near in range(NEAR):
                to = (x * ROWS_Y + pair) * tile
                if apart:
                    to = pl.multiple_of((near ^ place_ref[1]) * (PAIRS * tile) + to, tile)
                else:
                    to += near * PAIRS * tile
                row = pair * rows + near * tile
                for y in range(ROWS_Y):
                    for k in range(ROWS_X):
                        at = ((x ^ k) * ROWS_Y + y) * columns
                        queries[pl.ds(to, tile), at : at + columns] = parts_ref[
                            x * ROWS_Y + y, row : row + tile, k * columns : (k + 1) * columns
                        ]

    out_copies = []
    for n, copy in enumerate(copies):
        copy.wait()
        span = slice(n * examples, (n + 1) * examples)
        term = lax.dot_general(
            queries[...], held[span, :], (((1,), (1,)), ((), ())),
            preferred_element_type=jnp.float32,
        ).astype(terms.dtype)
        for k in range(NEAR):
            entries = term[k * PAIRS * tile : (k + 1) * PAIRS * tile]
            if apart:
                out_refs[k][:, span] = entries
            else:
                terms[k, :, span] = entries
        if not apart:
            span = pl.ds(n * examples, examples)
            out_copies.append(
                pltpu.make_async_copy(terms.at[:, :, span], out_refs[0].at[:, :, span], sent.at[n])
            )
            out_copies[-1].start()
    for copy in out_copies:
        copy.wait()


def scores_of(apart, place, parts, store):
    chips, block_rows, columns = parts.shape
    rows = ROWS_X * block_rows
    examples, width = store.shape
    steps = 4
    whole = (NEAR, rows // NEAR, examples)
    if apart:
        out_specs = [pl.BlockSpec(memory_space=pltpu.VMEM)] * NEAR
        out_shape = [jax.ShapeDtypeStruct(whole[1:], jnp.bfloat16)] * NEAR
    else:
        out_specs = [pl.BlockSpec(memory_space=pltpu.HBM)]
        out_shape = [pltpu.HBM(whole, jnp.bfloat16)]
    return pl.pallas_call(
        functools.partial(score, apart),
        in_specs=[
            pl.BlockSpec(memory_space=pltpu.SMEM),
            pl.BlockSpec(memory_space=pltpu.VMEM),
            pl.BlockSpec(memory_space=pltpu.HBM),
        ],
        out_specs=out_specs,
        out_shape=out_shape,
        scratch_shapes=[
            pltpu.VMEM((rows, width), jnp.bfloat16),
            pltpu.VMEM((examples, width), jnp.bfloat16),
            pltpu.SemaphoreType.DMA((steps,)),
            pltpu.VMEM((NEAR, 16, 128) if apart else whole, jnp.bfloat16),
            pltpu.SemaphoreType.DMA((steps,)),
        ],
        compiler_params=pltpu.CompilerParams(vmem_limit_bytes=50 * MIB),
        cost_estimate=pl.CostEstimate(
            flops=2 * rows * width * examples,
            bytes_accessed=2 * (rows * width + (width + rows) * examples),
            transcendentals=0,
        ),
    )(place, parts, store)


def add(place_ref, gathered_ref, *refs):
    other_refs, out_ref = refs[:-1], refs[-1]
    tile = out_ref.shape[1]
    sums = gathered_ref[0].astype(jnp.float32), other_refs[0][...].astype(jnp.float32)
    for k in range(1, NEAR):
        sums = (
            sums[0] + gathered_ref[k].astype(jnp.float32),
            sums[1] + other_refs[k][...].astype(jnp.float32),
        )
    for i, total in enumerate(sums):
        for p in range(out_ref.shape[0] // CORES):
            at = p * CORES + (place_ref[0] ^ i)
            out_ref[at] = total[p * tile : (p + 1) * tile].astype(out_ref.dtype)


def added(place, tile, gathered, others):
    steps = 4
    rows, examples = others[0].shape
    return pl.pallas_call(
        add,
        grid_spec=pltpu.PrefetchScalarGridSpec(
            num_scalar_prefetch=1,
            grid=(steps,),
            in_specs=[pl.BlockSpec((NEAR, rows // steps, examples), lambda s, place_ref: (0, s, 0))]
            + [pl.BlockSpec((rows // steps, examples), lambda s, place_ref: (s, 0))] * NEAR,
            out_specs=pl.BlockSpec(
                (PAIRS * CORES // steps, tile, examples), lambda s, place_ref: (s, 0, 0)
            ),
        ),
        out_shape=jax.ShapeDtypeStruct((PAIRS * CORES, tile, examples), jnp.bfloat16),
        compiler_params=pltpu.CompilerParams(vmem_limit_bytes=16 * MIB),
        cost_estimate=pl.CostEstimate(
            flops=2 * NEAR * rows * examples,
            bytes_accessed=6 * NEAR * rows * examples,
            transcendentals=0,
        ),
    )(place, gathered, *others)


def shards(query_grads, precond, codes, scales):
    own_queries, width = query_grads.shape
    examples = codes.shape[0]
    ex_size, slots = lax.axis_size("ex"), lax.axis_size("dim")
    tile = own_queries * ex_size // slots // CORES
    chips = ROWS_X * ROWS_Y
    position = lax.axis_index("ex")
    near_here = lax.axis_index("dim") % NEAR
    place = jnp.stack([position % CORES, near_here])
    spots = [(x, y, c) for x in range(ROWS_X) for y in range(ROWS_Y) for c in range(CORES)]

    def shift(x_by, y_by, core_by):
        return [
            (e, ((x + x_by) % ROWS_X * ROWS_Y + (y + y_by) % ROWS_Y) * CORES + (c + core_by) % CORES)
            for e, (x, y, c) in enumerate(spots)
        ]

    chip_group = ROWS_Y * CORES
    beside = [list(range(x * chip_group, (x + 1) * chip_group)) for x in range(ROWS_X)]
    same_core = [[chip * CORES + c for chip in range(chips)] for c in range(CORES)]
    near = [[pair * NEAR + i for i in range(NEAR)] for pair in range(PAIRS)]
    far = [
        [(chip * CORES + c) * slots + pair * NEAR + i for pair in range(PAIRS) for c in range(CORES)]
        for chip in range(chips)
        for i in range(NEAR)
    ]

    own, halves = precond[0], spread(query_grads, tile)
    own_other = lax.ppermute(own, "ex", shift(0, 0, 1))
    across = lax.ppermute(own, "ex", shift(1, 0, 0))
    mine = dequantized(codes, scales)
    across, mine = lax.optimization_barrier((across, mine))
    across_other = lax.ppermute(across, "ex", shift(0, 0, 1))

    grads = lax.all_to_all(
        halves, "ex", 0, 0, tiled=True, axis_index_groups=beside
    ).reshape(ROWS_Y * CORES * 2 * tile, width)

    grads, mine, own_other, across, across_other = lax.optimization_barrier(
        (grads, mine, own_other, across, across_other)
    )
    copies = conditioned_for(place, chips, grads, [own, own_other, across, across_other])
    mine, copies = lax.optimization_barrier((mine, copies))
    theirs = lax.ppermute(mine, "ex", shift(0, 0, 1))
    parts = lax.all_to_all(copies, "ex", 0, 0, tiled=True, axis_index_groups=same_core)

    (terms,) = scores_of(False, place, parts, mine)
    gathered = lax.all_to_all(terms, "dim", 0, 0, tiled=True, axis_index_groups=near)
    here, *away = scores_of(True, place, parts, theirs)
    others = [here] + [
        lax.ppermute(term, "dim", [(d, d ^ k) for d in range(slots)]) for k, term in enumerate(away, 1)
    ]
    sums = lax.all_to_all(
        added(place, tile, gathered, others), ("ex", "dim"), 0, 0, tiled=True, axis_index_groups=far
    )
    total = jnp.sum(sums.astype(jnp.float32).reshape(PAIRS, CORES * tile, examples), axis=0)
    return total * float(width * slots) ** (-0.5)


def solution(mesh):
    placed = (P("ex", "dim"), P("dim", None, "ex"), P("ex", "dim"), P("ex", "dim"))
    return jax.shard_map(
        shards, mesh=mesh, in_specs=placed, out_specs=P("dim", "ex"), check_vma=False
    )
```

```python
import functools

import jax
import jax.numpy as jnp
from jax import lax
from jax.experimental import pallas as pl
from jax.experimental.pallas import tpu as pltpu
from jax.sharding import PartitionSpec as P

CORES, ROWS_Y, ROWS_X = 2, 4, 2
PAIRS, SIDES = 8, 2
NEAR = 2 * SIDES
MIB = 1 << 20


def dequantize(codes_ref, scales_ref, out_ref):
    block = codes_ref.shape[1] // scales_ref.shape[1]
    for b in range(scales_ref.shape[1]):
        columns = slice(b * block, (b + 1) * block)
        entries = codes_ref[:, columns].astype(jnp.float32) * scales_ref[:, b : b + 1]
        out_ref[:, columns] = entries.astype(out_ref.dtype)


def dequantized(codes, scales):
    rows, width = codes.shape
    tile = 256
    return pl.pallas_call(
        dequantize,
        grid=(rows // tile,),
        in_specs=[
            pl.BlockSpec((tile, width), lambda r: (r, 0)),
            pl.BlockSpec((tile, scales.shape[1]), lambda r: (r, 0)),
        ],
        out_specs=pl.BlockSpec((tile, width), lambda r: (r, 0)),
        out_shape=jax.ShapeDtypeStruct(codes.shape, jnp.bfloat16),
        compiler_params=pltpu.CompilerParams(vmem_limit_bytes=56 * MIB),
        cost_estimate=pl.CostEstimate(
            flops=rows * width, bytes_accessed=4 * rows * width, transcendentals=0
        ),
    )(codes, scales)


def copy_halves(grads_ref, out_ref):
    tile = out_ref.shape[1] // 2
    for b in range(2):
        for core in range(CORES):
            row = (b * CORES + core) * tile
            entries = grads_ref[row : row + tile, :]
            for y in range(ROWS_Y):
                out_ref[y * CORES + core, b * tile : (b + 1) * tile, :] = entries


def spread(grads, tile):
    rows, width = grads.shape
    return pl.pallas_call(
        copy_halves,
        in_specs=[pl.BlockSpec(memory_space=pltpu.VMEM)],
        out_specs=pl.BlockSpec(memory_space=pltpu.VMEM),
        out_shape=jax.ShapeDtypeStruct((ROWS_Y * CORES, 2 * tile, width), grads.dtype),
        compiler_params=pltpu.CompilerParams(vmem_limit_bytes=8 * MIB),
        cost_estimate=pl.CostEstimate(
            flops=0, bytes_accessed=2 * (1 + ROWS_Y) * rows * width, transcendentals=0
        ),
    )(grads)


def condition(place_ref, *refs):
    grads_ref, column_refs, (parts_ref, weights) = refs[0], refs[1:-2], refs[-2:]
    columns = column_refs[0].shape[1]
    for core in range(CORES):

        @pl.when(place_ref[0] == core)
        def _():
            for i, ref in enumerate(column_refs):
                at = (i ^ core) * columns
                weights[:, at : at + columns] = ref[...]

    part = jnp.dot(grads_ref[...], weights[...], preferred_element_type=jnp.float32)
    for chip in range(parts_ref.shape[0]):
        parts_ref[chip] = part.astype(parts_ref.dtype)


def conditioned_for(place, chips, grads, columns):
    rows, width = grads.shape
    out = len(columns) * columns[0].shape[1]
    return pl.pallas_call(
        condition,
        in_specs=[pl.BlockSpec(memory_space=pltpu.SMEM)]
        + [pl.BlockSpec(memory_space=pltpu.VMEM)] * (1 + len(columns)),
        out_specs=pl.BlockSpec(memory_space=pltpu.VMEM),
        out_shape=jax.ShapeDtypeStruct((chips, rows, out), jnp.bfloat16),
        scratch_shapes=[pltpu.VMEM((width, out), jnp.bfloat16)],
        compiler_params=pltpu.CompilerParams(vmem_limit_bytes=16 * MIB),
        cost_estimate=pl.CostEstimate(
            flops=2 * rows * width * out,
            bytes_accessed=2 * (rows * width + width * out + chips * rows * out),
            transcendentals=0,
        ),
    )(place, grads, *columns)


def score(apart, place_ref, parts_ref, store_ref, *refs):
    out_refs, queries = refs[:-1], refs[-1]
    block_rows, columns = parts_ref.shape[1], parts_ref.shape[2] // ROWS_X
    rows = block_rows // ROWS_Y
    tile = rows // NEAR

    @pl.when(pl.program_id(0) == 0)
    def _():
        for x in range(ROWS_X):
            for pair in range(ROWS_Y):
                for near in range(NEAR):
                    to = (x * ROWS_Y + pair) * tile
                    if apart:
                        to = pl.multiple_of((near ^ place_ref[1]) * (PAIRS * tile) + to, tile)
                    else:
                        to += near * PAIRS * tile
                    row = pair * rows + near * tile
                    for y in range(ROWS_Y):
                        for k in range(ROWS_X):
                            at = ((x ^ k) * ROWS_Y + y) * columns
                            queries[pl.ds(to, tile), at : at + columns] = parts_ref[
                                x * ROWS_Y + y, row : row + tile, k * columns : (k + 1) * columns
                            ]

    term = lax.dot_general(
        queries[...], store_ref[...], (((1,), (1,)), ((), ())),
        preferred_element_type=jnp.float32,
    )
    for k in range(NEAR):
        entries = term[k * PAIRS * tile : (k + 1) * PAIRS * tile].astype(out_refs[0].dtype)
        if apart:
            out_refs[k][...] = entries
        else:
            out_refs[0][k] = entries


def scores_of(apart, place, parts, store):
    chips, block_rows, columns = parts.shape
    rows = ROWS_X * block_rows
    examples, width = store.shape
    tile = 256
    if apart:
        block, index, shape, count = (rows // NEAR, tile), lambda n, place_ref: (0, n), (rows // NEAR, examples), NEAR
    else:
        block, index = (NEAR, rows // NEAR, tile), lambda n, place_ref: (0, 0, n)
        shape, count = (NEAR, rows // NEAR, examples), 1
    return pl.pallas_call(
        functools.partial(score, apart),
        grid_spec=pltpu.PrefetchScalarGridSpec(
            num_scalar_prefetch=1,
            grid=(examples // tile,),
            in_specs=[
                pl.BlockSpec((chips, block_rows, columns), lambda n, place_ref: (0, 0, 0)),
                pl.BlockSpec((tile, width), lambda n, place_ref: (n, 0)),
            ],
            out_specs=[pl.BlockSpec(block, index)] * count,
            scratch_shapes=[pltpu.VMEM((rows, width), jnp.bfloat16)],
        ),
        out_shape=[jax.ShapeDtypeStruct(shape, jnp.bfloat16) if apart else pltpu.HBM(shape, jnp.bfloat16)] * count,
        compiler_params=pltpu.CompilerParams(vmem_limit_bytes=50 * MIB),
        cost_estimate=pl.CostEstimate(
            flops=2 * rows * width * examples,
            bytes_accessed=2 * (rows * width + (width + rows) * examples),
            transcendentals=0,
        ),
    )(place, parts, store)


def add(place_ref, gathered_ref, *refs):
    other_refs, out_ref = refs[:-1], refs[-1]
    tile = out_ref.shape[1]
    sums = gathered_ref[0].astype(jnp.float32), other_refs[0][...].astype(jnp.float32)
    for k in range(1, NEAR):
        sums = (
            sums[0] + gathered_ref[k].astype(jnp.float32),
            sums[1] + other_refs[k][...].astype(jnp.float32),
        )
    for i, total in enumerate(sums):
        for p in range(out_ref.shape[0] // CORES):
            at = p * CORES + (place_ref[0] ^ i)
            out_ref[at] = total[p * tile : (p + 1) * tile].astype(out_ref.dtype)


def added(place, tile, gathered, others):
    steps = 4
    rows, examples = others[0].shape
    return pl.pallas_call(
        add,
        grid_spec=pltpu.PrefetchScalarGridSpec(
            num_scalar_prefetch=1,
            grid=(steps,),
            in_specs=[pl.BlockSpec((NEAR, rows // steps, examples), lambda s, place_ref: (0, s, 0))]
            + [pl.BlockSpec((rows // steps, examples), lambda s, place_ref: (s, 0))] * NEAR,
            out_specs=pl.BlockSpec(
                (PAIRS * CORES // steps, tile, examples), lambda s, place_ref: (s, 0, 0)
            ),
        ),
        out_shape=jax.ShapeDtypeStruct((PAIRS * CORES, tile, examples), jnp.bfloat16),
        compiler_params=pltpu.CompilerParams(vmem_limit_bytes=16 * MIB),
        cost_estimate=pl.CostEstimate(
            flops=2 * NEAR * rows * examples,
            bytes_accessed=6 * NEAR * rows * examples,
            transcendentals=0,
        ),
    )(place, gathered, *others)


def shards(query_grads, precond, codes, scales):
    own_queries, width = query_grads.shape
    examples = codes.shape[0]
    ex_size, slots = lax.axis_size("ex"), lax.axis_size("dim")
    tile = own_queries * ex_size // slots // CORES
    chips = ROWS_X * ROWS_Y
    position = lax.axis_index("ex")
    near_here = lax.axis_index("dim") % NEAR
    place = jnp.stack([position % CORES, near_here])
    spots = [(x, y, c) for x in range(ROWS_X) for y in range(ROWS_Y) for c in range(CORES)]

    def shift(x_by, y_by, core_by):
        return [
            (e, ((x + x_by) % ROWS_X * ROWS_Y + (y + y_by) % ROWS_Y) * CORES + (c + core_by) % CORES)
            for e, (x, y, c) in enumerate(spots)
        ]

    chip_group = ROWS_Y * CORES
    beside = [list(range(x * chip_group, (x + 1) * chip_group)) for x in range(ROWS_X)]
    same_core = [[chip * CORES + c for chip in range(chips)] for c in range(CORES)]
    near = [[pair * NEAR + i for i in range(NEAR)] for pair in range(PAIRS)]
    far = [
        [(chip * CORES + c) * slots + pair * NEAR + i for pair in range(PAIRS) for c in range(CORES)]
        for chip in range(chips)
        for i in range(NEAR)
    ]

    own, halves = precond[0], spread(query_grads, tile)
    own_other = lax.ppermute(own, "ex", shift(0, 0, 1))
    across = lax.ppermute(own, "ex", shift(1, 0, 0))
    mine = dequantized(codes, scales)
    across, mine = lax.optimization_barrier((across, mine))
    across_other = lax.ppermute(across, "ex", shift(0, 0, 1))

    grads = lax.all_to_all(
        halves, "ex", 0, 0, tiled=True, axis_index_groups=beside
    ).reshape(ROWS_Y * CORES * 2 * tile, width)

    grads, mine, own_other, across, across_other = lax.optimization_barrier(
        (grads, mine, own_other, across, across_other)
    )
    copies = conditioned_for(place, chips, grads, [own, own_other, across, across_other])
    mine, copies = lax.optimization_barrier((mine, copies))
    theirs = lax.ppermute(mine, "ex", shift(0, 0, 1))
    parts = lax.all_to_all(copies, "ex", 0, 0, tiled=True, axis_index_groups=same_core)

    (terms,) = scores_of(False, place, parts, mine)
    gathered = lax.all_to_all(terms, "dim", 0, 0, tiled=True, axis_index_groups=near)
    here, *away = scores_of(True, place, parts, theirs)
    others = [here] + [
        lax.ppermute(
            term, "dim", [(d, (((d + SIDES) ^ k) - SIDES) % slots if k & SIDES else d ^ k) for d in range(slots)]
        )
        for k, term in enumerate(away, 1)
    ]
    sums = lax.all_to_all(
        added(place, tile, gathered, others), ("ex", "dim"), 0, 0, tiled=True, axis_index_groups=far
    )
    total = jnp.sum(sums.astype(jnp.float32).reshape(PAIRS, CORES * tile, examples), axis=0)
    return total * float(width * slots) ** (-0.5)


def solution(mesh):
    placed = (P("ex", "dim"), P("dim", None, "ex"), P("ex", "dim"), P("ex", "dim"))
    return jax.shard_map(
        shards, mesh=mesh, in_specs=placed, out_specs=P("dim", "ex"), check_vma=False
    )
```

```python
import functools

import jax
import jax.numpy as jnp
from jax import lax
from jax.experimental import pallas as pl
from jax.experimental.pallas import tpu as pltpu
from jax.sharding import PartitionSpec as P

CORES, ROWS_Y, ROWS_X = 2, 4, 2
PAIRS, SIDES = 8, 2
NEAR = 2 * SIDES
MIB = 1 << 20


def dequantize(codes_ref, scales_ref, out_ref):
    block = codes_ref.shape[1] // scales_ref.shape[1]
    for b in range(scales_ref.shape[1]):
        columns = slice(b * block, (b + 1) * block)
        entries = codes_ref[:, columns].astype(jnp.float32) * scales_ref[:, b : b + 1]
        out_ref[:, columns] = entries.astype(out_ref.dtype)


def dequantized(codes, scales):
    rows, width = codes.shape
    tile = 256
    return pl.pallas_call(
        dequantize,
        grid=(rows // tile,),
        in_specs=[
            pl.BlockSpec((tile, width), lambda r: (r, 0)),
            pl.BlockSpec((tile, scales.shape[1]), lambda r: (r, 0)),
        ],
        out_specs=pl.BlockSpec((tile, width), lambda r: (r, 0)),
        out_shape=jax.ShapeDtypeStruct(codes.shape, jnp.bfloat16),
        compiler_params=pltpu.CompilerParams(vmem_limit_bytes=56 * MIB),
        cost_estimate=pl.CostEstimate(
            flops=rows * width, bytes_accessed=4 * rows * width, transcendentals=0
        ),
    )(codes, scales)


def copy_halves(grads_ref, out_ref):
    tile = out_ref.shape[1] // 2
    for b in range(2):
        for core in range(CORES):
            row = (b * CORES + core) * tile
            entries = grads_ref[row : row + tile, :]
            for y in range(ROWS_Y):
                out_ref[y * CORES + core, b * tile : (b + 1) * tile, :] = entries


def spread(grads, tile):
    rows, width = grads.shape
    return pl.pallas_call(
        copy_halves,
        in_specs=[pl.BlockSpec(memory_space=pltpu.VMEM)],
        out_specs=pl.BlockSpec(memory_space=pltpu.VMEM),
        out_shape=jax.ShapeDtypeStruct((ROWS_Y * CORES, 2 * tile, width), grads.dtype),
        compiler_params=pltpu.CompilerParams(vmem_limit_bytes=8 * MIB),
        cost_estimate=pl.CostEstimate(
            flops=0, bytes_accessed=2 * (1 + ROWS_Y) * rows * width, transcendentals=0
        ),
    )(grads)


def condition(place_ref, *refs):
    grads_ref, column_refs, (parts_ref, weights) = refs[0], refs[1:-2], refs[-2:]
    columns = column_refs[0].shape[1]
    for core in range(CORES):

        @pl.when(place_ref[0] == core)
        def _():
            for i, ref in enumerate(column_refs):
                at = (i ^ core) * columns
                weights[:, at : at + columns] = ref[...]

    part = jnp.dot(grads_ref[...], weights[...], preferred_element_type=jnp.float32)
    for chip in range(parts_ref.shape[0]):
        parts_ref[chip] = part.astype(parts_ref.dtype)


def conditioned_for(place, chips, grads, columns):
    rows, width = grads.shape
    out = len(columns) * columns[0].shape[1]
    return pl.pallas_call(
        condition,
        in_specs=[pl.BlockSpec(memory_space=pltpu.SMEM)]
        + [pl.BlockSpec(memory_space=pltpu.VMEM)] * (1 + len(columns)),
        out_specs=pl.BlockSpec(memory_space=pltpu.VMEM),
        out_shape=jax.ShapeDtypeStruct((chips, rows, out), jnp.bfloat16),
        scratch_shapes=[pltpu.VMEM((width, out), jnp.bfloat16)],
        compiler_params=pltpu.CompilerParams(vmem_limit_bytes=16 * MIB),
        cost_estimate=pl.CostEstimate(
            flops=2 * rows * width * out,
            bytes_accessed=2 * (rows * width + width * out + chips * rows * out),
            transcendentals=0,
        ),
    )(place, grads, *columns)


def score(apart, place_ref, parts_ref, store_ref, *refs):
    out_refs, queries = refs[:-1], refs[-1]
    block_rows, columns = parts_ref.shape[1], parts_ref.shape[2] // ROWS_X
    rows = block_rows // ROWS_Y
    tile = rows // NEAR

    @pl.when(pl.program_id(0) == 0)
    def _():
        for x in range(ROWS_X):
            for pair in range(ROWS_Y):
                for near in range(NEAR):
                    to = (x * ROWS_Y + pair) * tile
                    if apart:
                        to = pl.multiple_of((near ^ place_ref[1]) * (PAIRS * tile) + to, tile)
                    else:
                        to += near * PAIRS * tile
                    row = pair * rows + near * tile
                    for y in range(ROWS_Y):
                        for k in range(ROWS_X):
                            at = ((x ^ k) * ROWS_Y + y) * columns
                            queries[pl.ds(to, tile), at : at + columns] = parts_ref[
                                x * ROWS_Y + y, row : row + tile, k * columns : (k + 1) * columns
                            ]

    term = lax.dot_general(
        queries[...], store_ref[...], (((1,), (1,)), ((), ())),
        preferred_element_type=jnp.float32,
    )
    for k in range(NEAR):
        entries = term[k * PAIRS * tile : (k + 1) * PAIRS * tile].astype(out_refs[0].dtype)
        if apart:
            out_refs[k][...] = entries
        else:
            out_refs[0][k] = entries


def scores_of(apart, place, parts, store):
    chips, block_rows, columns = parts.shape
    rows = ROWS_X * block_rows
    examples, width = store.shape
    tile = 256
    if apart:
        block, index, shape, count = (rows // NEAR, tile), lambda n, place_ref: (0, n), (rows // NEAR, examples), NEAR
    else:
        block, index = (NEAR, rows // NEAR, tile), lambda n, place_ref: (0, 0, n)
        shape, count = (NEAR, rows // NEAR, examples), 1
    return pl.pallas_call(
        functools.partial(score, apart),
        grid_spec=pltpu.PrefetchScalarGridSpec(
            num_scalar_prefetch=1,
            grid=(examples // tile,),
            in_specs=[
                pl.BlockSpec((chips, block_rows, columns), lambda n, place_ref: (0, 0, 0)),
                pl.BlockSpec((tile, width), lambda n, place_ref: (n, 0)),
            ],
            out_specs=[pl.BlockSpec(block, index)] * count,
            scratch_shapes=[pltpu.VMEM((rows, width), jnp.bfloat16)],
        ),
        out_shape=[jax.ShapeDtypeStruct(shape, jnp.bfloat16) if apart else pltpu.HBM(shape, jnp.bfloat16)] * count,
        compiler_params=pltpu.CompilerParams(vmem_limit_bytes=50 * MIB),
        cost_estimate=pl.CostEstimate(
            flops=2 * rows * width * examples,
            bytes_accessed=2 * (rows * width + (width + rows) * examples),
            transcendentals=0,
        ),
    )(place, parts, store)


def split(place_ref, *refs):
    terms, kept_ref, sent_ref = refs[:-2], refs[-2], refs[-1]
    for i, out_ref in enumerate((kept_ref, sent_ref)):
        blocks = terms[i::2]
        if len(blocks) == 1:
            blocks = [blocks[0].at[k] for k in range(NEAR)]
        total = blocks[0][...].astype(jnp.float32)
        for block in blocks[1:]:
            total += block[...].astype(jnp.float32)
        out_ref[...] = total.astype(out_ref.dtype)


def split_sums(place, tile, terms):
    half = PAIRS // 2
    examples = terms[0].shape[-1]

    def spec(ndim, flip):
        def rows(j, place_ref):
            return 2 * j + (1 - place_ref[2] if flip else place_ref[2])

        if ndim == 2:
            return pl.BlockSpec((tile, examples), lambda j, place_ref: (rows(j, place_ref), 0))
        return pl.BlockSpec((NEAR, tile, examples), lambda j, place_ref: (0, rows(j, place_ref), 0))

    return pl.pallas_call(
        split,
        grid_spec=pltpu.PrefetchScalarGridSpec(
            num_scalar_prefetch=1,
            grid=(half,),
            in_specs=[spec(term.ndim, flip) for term in terms for flip in (False, True)],
            out_specs=[pl.BlockSpec((pl.squeezed, tile, examples), lambda j, place_ref: (j, 0, 0))] * 2,
        ),
        out_shape=[
            jax.ShapeDtypeStruct((half, tile, examples), jnp.float32),
            jax.ShapeDtypeStruct((half, tile, examples), jnp.bfloat16),
        ],
        compiler_params=pltpu.CompilerParams(vmem_limit_bytes=16 * MIB),
        cost_estimate=pl.CostEstimate(
            flops=2 * NEAR * half * tile * examples,
            bytes_accessed=5 * NEAR * half * tile * examples,
            transcendentals=0,
        ),
    )(place, *[term for term in terms for _ in range(2)])


def join(place_ref, *refs):
    out_ref = refs[-1]
    for i in range(CORES):
        kept_ref, came_ref = refs[2 * i], refs[2 * i + 1]
        for j in range(kept_ref.shape[0]):
            total = kept_ref[j] + came_ref[j].astype(jnp.float32)
            out_ref[j * CORES + (place_ref[0] ^ i)] = total.astype(out_ref.dtype)


def joined(place, *halves):
    pairs, tile, examples = halves[0].shape
    return pl.pallas_call(
        join,
        in_specs=[pl.BlockSpec(memory_space=pltpu.SMEM)]
        + [pl.BlockSpec(memory_space=pltpu.VMEM)] * len(halves),
        out_specs=pl.BlockSpec(memory_space=pltpu.VMEM),
        out_shape=jax.ShapeDtypeStruct((pairs * CORES, tile, examples), jnp.bfloat16),
        compiler_params=pltpu.CompilerParams(vmem_limit_bytes=16 * MIB),
        cost_estimate=pl.CostEstimate(
            flops=CORES * pairs * tile * examples,
            bytes_accessed=8 * CORES * pairs * tile * examples,
            transcendentals=0,
        ),
    )(place, *halves)


def shards(query_grads, precond, codes, scales):
    own_queries, width = query_grads.shape
    examples = codes.shape[0]
    ex_size, slots = lax.axis_size("ex"), lax.axis_size("dim")
    tile = own_queries * ex_size // slots // CORES
    chips = ROWS_X * ROWS_Y
    position = lax.axis_index("ex")
    slot = lax.axis_index("dim")
    place = jnp.stack([position % CORES, slot % NEAR, slot // NEAR % 2])
    spots = [(x, y, c) for x in range(ROWS_X) for y in range(ROWS_Y) for c in range(CORES)]

    def shift(x_by, y_by, core_by):
        return [
            (e, ((x + x_by) % ROWS_X * ROWS_Y + (y + y_by) % ROWS_Y) * CORES + (c + core_by) % CORES)
            for e, (x, y, c) in enumerate(spots)
        ]

    chip_group = ROWS_Y * CORES
    beside = [list(range(x * chip_group, (x + 1) * chip_group)) for x in range(ROWS_X)]
    same_core = [[chip * CORES + c for chip in range(chips)] for c in range(CORES)]
    near = [[pair * NEAR + i for i in range(NEAR)] for pair in range(PAIRS)]
    far = [
        [(chip * CORES + c) * slots + pair * NEAR + i for pair in range(parity, PAIRS, 2) for c in range(CORES)]
        for chip in range(chips)
        for i in range(NEAR)
        for parity in range(2)
    ]

    own, halves = precond[0], spread(query_grads, tile)
    own_other = lax.ppermute(own, "ex", shift(0, 0, 1))
    across = lax.ppermute(own, "ex", shift(1, 0, 0))
    mine = dequantized(codes, scales)
    across, mine = lax.optimization_barrier((across, mine))
    across_other = lax.ppermute(across, "ex", shift(0, 0, 1))

    grads = lax.all_to_all(
        halves, "ex", 0, 0, tiled=True, axis_index_groups=beside
    ).reshape(ROWS_Y * CORES * 2 * tile, width)

    grads, mine, own_other, across, across_other = lax.optimization_barrier(
        (grads, mine, own_other, across, across_other)
    )
    copies = conditioned_for(place, chips, grads, [own, own_other, across, across_other])
    mine, copies = lax.optimization_barrier((mine, copies))
    theirs = lax.ppermute(mine, "ex", shift(0, 0, 1))
    parts = lax.all_to_all(copies, "ex", 0, 0, tiled=True, axis_index_groups=same_core)

    (terms,) = scores_of(False, place, parts, mine)
    gathered = lax.all_to_all(terms, "dim", 0, 0, tiled=True, axis_index_groups=near)
    here, *away = scores_of(True, place, parts, theirs)
    others = [here] + [
        lax.ppermute(
            term, "dim", [(d, (((d + SIDES) ^ k) - SIDES) % slots if k & SIDES else d ^ k) for d in range(slots)]
        )
        for k, term in enumerate(away, 1)
    ]
    kept, sent = split_sums(place, tile, [gathered])
    came = lax.ppermute(sent, "dim", [(d, d ^ NEAR) for d in range(slots)])
    *others, sent = lax.optimization_barrier((*others, sent))
    kept_other, sent_other = split_sums(place, tile, others)
    came_other = lax.ppermute(
        sent_other, "dim", [(d, (((d + NEAR) ^ NEAR) - NEAR) % slots) for d in range(slots)]
    )
    sums = lax.all_to_all(
        joined(place, kept, came, kept_other, came_other),
        ("ex", "dim"), 0, 0, tiled=True, axis_index_groups=far,
    )
    total = jnp.sum(sums.astype(jnp.float32).reshape(PAIRS // 2, CORES * tile, examples), axis=0)
    return total * float(width * slots) ** (-0.5)


def solution(mesh):
    placed = (P("ex", "dim"), P("dim", None, "ex"), P("ex", "dim"), P("ex", "dim"))
    return jax.shard_map(
        shards, mesh=mesh, in_specs=placed, out_specs=P("dim", "ex"), check_vma=False
    )
```

```python
import jax
import jax.numpy as jnp
from jax import lax
from jax.experimental import pallas as pl
from jax.experimental.pallas import tpu as pltpu
from jax.sharding import PartitionSpec as P

CORES, ROWS_Y, ROWS_X = 2, 4, 2
PAIRS, SIDES = 8, 2
NEAR = 2 * SIDES
MIB = 1 << 20


def dequantize(codes_ref, scales_ref, out_ref):
    block = codes_ref.shape[1] // scales_ref.shape[1]
    for b in range(scales_ref.shape[1]):
        columns = slice(b * block, (b + 1) * block)
        entries = codes_ref[:, columns].astype(jnp.float32) * scales_ref[:, b : b + 1]
        out_ref[:, columns] = entries.astype(out_ref.dtype)


def dequantized(codes, scales):
    rows, width = codes.shape
    tile = 256
    return pl.pallas_call(
        dequantize,
        grid=(rows // tile,),
        in_specs=[
            pl.BlockSpec((tile, width), lambda r: (r, 0)),
            pl.BlockSpec((tile, scales.shape[1]), lambda r: (r, 0)),
        ],
        out_specs=pl.BlockSpec((tile, width), lambda r: (r, 0)),
        out_shape=jax.ShapeDtypeStruct(codes.shape, jnp.bfloat16),
        compiler_params=pltpu.CompilerParams(vmem_limit_bytes=56 * MIB),
        cost_estimate=pl.CostEstimate(
            flops=rows * width, bytes_accessed=4 * rows * width, transcendentals=0
        ),
    )(codes, scales)


def copy_halves(grads_ref, out_ref):
    tile = out_ref.shape[1] // 2
    for b in range(2):
        for core in range(CORES):
            row = (b * CORES + core) * tile
            entries = grads_ref[row : row + tile, :]
            for y in range(ROWS_Y):
                out_ref[y * CORES + core, b * tile : (b + 1) * tile, :] = entries


def spread(grads, tile):
    rows, width = grads.shape
    return pl.pallas_call(
        copy_halves,
        in_specs=[pl.BlockSpec(memory_space=pltpu.VMEM)],
        out_specs=pl.BlockSpec(memory_space=pltpu.VMEM),
        out_shape=jax.ShapeDtypeStruct((ROWS_Y * CORES, 2 * tile, width), grads.dtype),
        compiler_params=pltpu.CompilerParams(vmem_limit_bytes=8 * MIB),
        cost_estimate=pl.CostEstimate(
            flops=0, bytes_accessed=2 * (1 + ROWS_Y) * rows * width, transcendentals=0
        ),
    )(grads)


def condition(place_ref, *refs):
    grads_ref, column_refs, (parts_ref, weights) = refs[0], refs[1:-2], refs[-2:]
    columns = column_refs[0].shape[1]
    for core in range(CORES):

        @pl.when(place_ref[0] == core)
        def _():
            for i, ref in enumerate(column_refs):
                at = (i ^ core) * columns
                weights[:, at : at + columns] = ref[...]

    part = jnp.dot(grads_ref[...], weights[...], preferred_element_type=jnp.float32)
    for chip in range(parts_ref.shape[0]):
        parts_ref[chip] = part.astype(parts_ref.dtype)


def conditioned_for(place, chips, grads, columns):
    rows, width = grads.shape
    out = len(columns) * columns[0].shape[1]
    return pl.pallas_call(
        condition,
        in_specs=[pl.BlockSpec(memory_space=pltpu.SMEM)]
        + [pl.BlockSpec(memory_space=pltpu.VMEM)] * (1 + len(columns)),
        out_specs=pl.BlockSpec(memory_space=pltpu.VMEM),
        out_shape=jax.ShapeDtypeStruct((chips, rows, out), jnp.bfloat16),
        scratch_shapes=[pltpu.VMEM((width, out), jnp.bfloat16)],
        compiler_params=pltpu.CompilerParams(vmem_limit_bytes=16 * MIB),
        cost_estimate=pl.CostEstimate(
            flops=2 * rows * width * out,
            bytes_accessed=2 * (rows * width + width * out + chips * rows * out),
            transcendentals=0,
        ),
    )(place, grads, *columns)


def score(place_ref, parts_ref, mine_ref, theirs_ref, out_ref, *refs):
    apart_refs, queries = refs[:-1], refs[-1]
    block_rows, columns = parts_ref.shape[1], parts_ref.shape[2] // ROWS_X
    rows = block_rows // ROWS_Y
    tile = rows // NEAR

    @pl.when(pl.program_id(0) == 0)
    def _():
        for x in range(ROWS_X):
            for pair in range(ROWS_Y):
                for near in range(NEAR):
                    to = (near ^ place_ref[1]) * (PAIRS * tile) + (x * ROWS_Y + pair) * tile
                    to = pl.multiple_of(to, tile)
                    row = pair * rows + near * tile
                    for y in range(ROWS_Y):
                        for k in range(ROWS_X):
                            at = ((x ^ k) * ROWS_Y + y) * columns
                            queries[pl.ds(to, tile), at : at + columns] = parts_ref[
                                x * ROWS_Y + y, row : row + tile, k * columns : (k + 1) * columns
                            ]

    def times(store_ref):
        term = lax.dot_general(
            queries[...], store_ref[...], (((1,), (1,)), ((), ())),
            preferred_element_type=jnp.float32,
        ).astype(out_ref.dtype)
        return [term[k * PAIRS * tile : (k + 1) * PAIRS * tile] for k in range(NEAR)]

    for k, entries in enumerate(times(mine_ref)):
        out_ref[k ^ place_ref[1]] = entries
    for ref, entries in zip(apart_refs, times(theirs_ref), strict=True):
        ref[...] = entries


def scores_of(place, parts, mine, theirs):
    chips, block_rows, columns = parts.shape
    rows = ROWS_X * block_rows
    examples, width = mine.shape
    tile = 256
    shape = (NEAR, rows // NEAR, examples)
    store_spec = pl.BlockSpec((tile, width), lambda n, place_ref: (n, 0))
    return pl.pallas_call(
        score,
        grid_spec=pltpu.PrefetchScalarGridSpec(
            num_scalar_prefetch=1,
            grid=(examples // tile,),
            in_specs=[
                pl.BlockSpec((chips, block_rows, columns), lambda n, place_ref: (0, 0, 0)),
                store_spec,
                store_spec,
            ],
            out_specs=[pl.BlockSpec((NEAR, rows // NEAR, tile), lambda n, place_ref: (0, 0, n))]
            + [pl.BlockSpec((rows // NEAR, tile), lambda n, place_ref: (0, n))] * NEAR,
            scratch_shapes=[pltpu.VMEM((rows, width), jnp.bfloat16)],
        ),
        out_shape=[pltpu.HBM(shape, jnp.bfloat16)]
        + [jax.ShapeDtypeStruct(shape[1:], jnp.bfloat16)] * NEAR,
        compiler_params=pltpu.CompilerParams(vmem_limit_bytes=32 * MIB),
        cost_estimate=pl.CostEstimate(
            flops=2 * CORES * rows * width * examples,
            bytes_accessed=2 * (rows * width + CORES * (width + rows) * examples),
            transcendentals=0,
        ),
    )(place, parts, mine, theirs)


def add(place_ref, gathered_ref, *refs):
    other_refs, out_ref = refs[:-1], refs[-1]
    tile = out_ref.shape[1]
    sums = gathered_ref[0].astype(jnp.float32), other_refs[0][...].astype(jnp.float32)
    for k in range(1, NEAR):
        sums = (
            sums[0] + gathered_ref[k].astype(jnp.float32),
            sums[1] + other_refs[k][...].astype(jnp.float32),
        )
    for i, total in enumerate(sums):
        for p in range(out_ref.shape[0] // CORES):
            at = p * CORES + (place_ref[0] ^ i)
            out_ref[at] = total[p * tile : (p + 1) * tile].astype(out_ref.dtype)


def added(place, tile, gathered, others):
    steps = 4
    rows, examples = others[0].shape
    return pl.pallas_call(
        add,
        grid_spec=pltpu.PrefetchScalarGridSpec(
            num_scalar_prefetch=1,
            grid=(steps,),
            in_specs=[pl.BlockSpec((NEAR, rows // steps, examples), lambda s, place_ref: (0, s, 0))]
            + [pl.BlockSpec((rows // steps, examples), lambda s, place_ref: (s, 0))] * NEAR,
            out_specs=pl.BlockSpec(
                (PAIRS * CORES // steps, tile, examples), lambda s, place_ref: (s, 0, 0)
            ),
        ),
        out_shape=jax.ShapeDtypeStruct((PAIRS * CORES, tile, examples), jnp.bfloat16),
        compiler_params=pltpu.CompilerParams(vmem_limit_bytes=16 * MIB),
        cost_estimate=pl.CostEstimate(
            flops=2 * NEAR * rows * examples,
            bytes_accessed=6 * NEAR * rows * examples,
            transcendentals=0,
        ),
    )(place, gathered, *others)


def shards(query_grads, precond, codes, scales):
    own_queries, width = query_grads.shape
    examples = codes.shape[0]
    ex_size, slots = lax.axis_size("ex"), lax.axis_size("dim")
    tile = own_queries * ex_size // slots // CORES
    chips = ROWS_X * ROWS_Y
    position = lax.axis_index("ex")
    near_here = lax.axis_index("dim") % NEAR
    place = jnp.stack([position % CORES, near_here])
    spots = [(x, y, c) for x in range(ROWS_X) for y in range(ROWS_Y) for c in range(CORES)]

    def shift(x_by, y_by, core_by):
        return [
            (e, ((x + x_by) % ROWS_X * ROWS_Y + (y + y_by) % ROWS_Y) * CORES + (c + core_by) % CORES)
            for e, (x, y, c) in enumerate(spots)
        ]

    chip_group = ROWS_Y * CORES
    beside = [list(range(x * chip_group, (x + 1) * chip_group)) for x in range(ROWS_X)]
    same_core = [[chip * CORES + c for chip in range(chips)] for c in range(CORES)]
    near = [[pair * NEAR + i for i in range(NEAR)] for pair in range(PAIRS)]
    far = [
        [(chip * CORES + c) * slots + pair * NEAR + i for pair in range(PAIRS) for c in range(CORES)]
        for chip in range(chips)
        for i in range(NEAR)
    ]

    own, halves = precond[0], spread(query_grads, tile)
    own_other = lax.ppermute(own, "ex", shift(0, 0, 1))
    across = lax.ppermute(own, "ex", shift(1, 0, 0))
    mine = dequantized(codes, scales)
    across, mine = lax.optimization_barrier((across, mine))
    across_other = lax.ppermute(across, "ex", shift(0, 0, 1))

    grads = lax.all_to_all(
        halves, "ex", 0, 0, tiled=True, axis_index_groups=beside
    ).reshape(ROWS_Y * CORES * 2 * tile, width)

    grads, mine, own_other, across, across_other = lax.optimization_barrier(
        (grads, mine, own_other, across, across_other)
    )
    copies = conditioned_for(place, chips, grads, [own, own_other, across, across_other])
    mine, copies = lax.optimization_barrier((mine, copies))
    theirs = lax.ppermute(mine, "ex", shift(0, 0, 1))
    parts = lax.all_to_all(copies, "ex", 0, 0, tiled=True, axis_index_groups=same_core)

    terms, here, *away = scores_of(place, parts, mine, theirs)
    gathered = lax.all_to_all(terms, "dim", 0, 0, tiled=True, axis_index_groups=near)
    others = [here] + [
        lax.ppermute(
            term, "dim", [(d, (((d + SIDES) ^ k) - SIDES) % slots if k & SIDES else d ^ k) for d in range(slots)]
        )
        for k, term in enumerate(away, 1)
    ]
    sums = lax.all_to_all(
        added(place, tile, gathered, others), ("ex", "dim"), 0, 0, tiled=True, axis_index_groups=far
    )
    total = jnp.sum(sums.astype(jnp.float32).reshape(PAIRS, CORES * tile, examples), axis=0)
    return total * float(width * slots) ** (-0.5)


def solution(mesh):
    placed = (P("ex", "dim"), P("dim", None, "ex"), P("ex", "dim"), P("ex", "dim"))
    return jax.shard_map(
        shards, mesh=mesh, in_specs=placed, out_specs=P("dim", "ex"), check_vma=False
    )
```

```python
import jax
import jax.numpy as jnp
from jax import lax
from jax.experimental import pallas as pl
from jax.experimental.pallas import tpu as pltpu
from jax.sharding import PartitionSpec as P

CORES, ROWS_Y, ROWS_X = 2, 4, 2
PAIRS, SIDES = 8, 2
NEAR = 2 * SIDES
MIB = 1 << 20


def dequantize(codes_ref, scales_ref, out_ref):
    block = codes_ref.shape[1] // scales_ref.shape[1]
    for b in range(scales_ref.shape[1]):
        columns = slice(b * block, (b + 1) * block)
        entries = codes_ref[:, columns].astype(jnp.float32) * scales_ref[:, b : b + 1]
        out_ref[:, columns] = entries.astype(out_ref.dtype)


def dequantized(codes, scales):
    rows, width = codes.shape
    tile = 256
    return pl.pallas_call(
        dequantize,
        grid=(rows // tile,),
        in_specs=[
            pl.BlockSpec((tile, width), lambda r: (r, 0)),
            pl.BlockSpec((tile, scales.shape[1]), lambda r: (r, 0)),
        ],
        out_specs=pl.BlockSpec((tile, width), lambda r: (r, 0)),
        out_shape=jax.ShapeDtypeStruct(codes.shape, jnp.bfloat16),
        compiler_params=pltpu.CompilerParams(vmem_limit_bytes=56 * MIB),
        cost_estimate=pl.CostEstimate(
            flops=rows * width, bytes_accessed=4 * rows * width, transcendentals=0
        ),
    )(codes, scales)


def copy_halves(grads_ref, out_ref):
    tile = out_ref.shape[1] // 2
    for b in range(2):
        for core in range(CORES):
            row = (b * CORES + core) * tile
            entries = grads_ref[row : row + tile, :]
            for y in range(ROWS_Y):
                out_ref[y * CORES + core, b * tile : (b + 1) * tile, :] = entries


def spread(grads, tile):
    rows, width = grads.shape
    return pl.pallas_call(
        copy_halves,
        in_specs=[pl.BlockSpec(memory_space=pltpu.VMEM)],
        out_specs=pl.BlockSpec(memory_space=pltpu.VMEM),
        out_shape=jax.ShapeDtypeStruct((ROWS_Y * CORES, 2 * tile, width), grads.dtype),
        compiler_params=pltpu.CompilerParams(vmem_limit_bytes=8 * MIB),
        cost_estimate=pl.CostEstimate(
            flops=0, bytes_accessed=2 * (1 + ROWS_Y) * rows * width, transcendentals=0
        ),
    )(grads)


def condition(place_ref, *refs):
    grads_ref, column_refs, (parts_ref, weights) = refs[0], refs[1:-2], refs[-2:]
    columns = column_refs[0].shape[1]
    for core in range(CORES):

        @pl.when(place_ref[0] == core)
        def _():
            for i, ref in enumerate(column_refs):
                at = (i ^ core) * columns
                weights[:, at : at + columns] = ref[...]

    part = jnp.dot(grads_ref[...], weights[...], preferred_element_type=jnp.float32)
    for chip in range(parts_ref.shape[0]):
        parts_ref[chip] = part.astype(parts_ref.dtype)


def conditioned_for(place, chips, grads, columns):
    rows, width = grads.shape
    out = len(columns) * columns[0].shape[1]
    return pl.pallas_call(
        condition,
        in_specs=[pl.BlockSpec(memory_space=pltpu.SMEM)]
        + [pl.BlockSpec(memory_space=pltpu.VMEM)] * (1 + len(columns)),
        out_specs=pl.BlockSpec(memory_space=pltpu.VMEM),
        out_shape=jax.ShapeDtypeStruct((chips, rows, out), jnp.bfloat16),
        scratch_shapes=[pltpu.VMEM((width, out), jnp.bfloat16)],
        compiler_params=pltpu.CompilerParams(vmem_limit_bytes=16 * MIB),
        cost_estimate=pl.CostEstimate(
            flops=2 * rows * width * out,
            bytes_accessed=2 * (rows * width + width * out + chips * rows * out),
            transcendentals=0,
        ),
    )(place, grads, *columns)


def score(place_ref, parts_ref, mine_ref, theirs_ref, out_ref, *refs):
    apart_refs, queries = refs[:-1], refs[-1]
    block_rows, columns = parts_ref.shape[1], parts_ref.shape[2] // ROWS_X
    rows = block_rows // ROWS_Y
    tile = rows // NEAR

    @pl.when(pl.program_id(0) == 0)
    def _():
        for x in range(ROWS_X):
            for pair in range(ROWS_Y):
                for near in range(NEAR):
                    to = (near ^ place_ref[1]) * (PAIRS * tile) + (x * ROWS_Y + pair) * tile
                    to = pl.multiple_of(to, tile)
                    row = pair * rows + near * tile
                    for y in range(ROWS_Y):
                        for k in range(ROWS_X):
                            at = ((x ^ k) * ROWS_Y + y) * columns
                            queries[pl.ds(to, tile), at : at + columns] = parts_ref[
                                x * ROWS_Y + y, row : row + tile, k * columns : (k + 1) * columns
                            ]

    def times(store_ref):
        term = lax.dot_general(
            queries[...], store_ref[...], (((1,), (1,)), ((), ())),
            preferred_element_type=jnp.float32,
        ).astype(out_ref.dtype)
        return [term[k * PAIRS * tile : (k + 1) * PAIRS * tile] for k in range(NEAR)]

    for k, entries in enumerate(times(mine_ref)):
        out_ref[k ^ place_ref[1]] = entries
    for k, entries in enumerate(times(theirs_ref)):
        apart_refs[k // SIDES][k % SIDES] = entries


def scores_of(place, parts, mine, theirs):
    chips, block_rows, columns = parts.shape
    rows = ROWS_X * block_rows
    examples, width = mine.shape
    tile = 256
    shape = (NEAR, rows // NEAR, examples)
    store_spec = pl.BlockSpec((tile, width), lambda n, place_ref: (n, 0))
    return pl.pallas_call(
        score,
        grid_spec=pltpu.PrefetchScalarGridSpec(
            num_scalar_prefetch=1,
            grid=(examples // tile,),
            in_specs=[
                pl.BlockSpec((chips, block_rows, columns), lambda n, place_ref: (0, 0, 0)),
                store_spec,
                store_spec,
            ],
            out_specs=[pl.BlockSpec((NEAR, rows // NEAR, tile), lambda n, place_ref: (0, 0, n))]
            + [pl.BlockSpec((SIDES, rows // NEAR, tile), lambda n, place_ref: (0, 0, n))] * 2,
            scratch_shapes=[pltpu.VMEM((rows, width), jnp.bfloat16)],
        ),
        out_shape=[pltpu.HBM(shape, jnp.bfloat16)]
        + [jax.ShapeDtypeStruct((SIDES,) + shape[1:], jnp.bfloat16)] * 2,
        compiler_params=pltpu.CompilerParams(vmem_limit_bytes=32 * MIB),
        cost_estimate=pl.CostEstimate(
            flops=2 * CORES * rows * width * examples,
            bytes_accessed=2 * (rows * width + CORES * (width + rows) * examples),
            transcendentals=0,
        ),
    )(place, parts, mine, theirs)


def fold(here_ref, came_ref, kept_ref, sent_ref):
    kept_ref[...] = here_ref[0].astype(jnp.float32) + came_ref[0].astype(jnp.float32)
    sent_ref[...] = (here_ref[1].astype(jnp.float32) + came_ref[1].astype(jnp.float32)).astype(sent_ref.dtype)


def folded(here, came):
    steps = 4
    sides, rows, examples = here.shape
    block = pl.BlockSpec((sides, rows // steps, examples), lambda s: (0, s, 0))
    return pl.pallas_call(
        fold,
        grid=(steps,),
        in_specs=[block, block],
        out_specs=[pl.BlockSpec((rows // steps, examples), lambda s: (s, 0))] * 2,
        out_shape=[jax.ShapeDtypeStruct((rows, examples), dtype) for dtype in (jnp.float32, jnp.bfloat16)],
        compiler_params=pltpu.CompilerParams(vmem_limit_bytes=16 * MIB),
        cost_estimate=pl.CostEstimate(
            flops=2 * rows * examples, bytes_accessed=14 * rows * examples, transcendentals=0
        ),
    )(here, came)


def add(place_ref, gathered_ref, *refs):
    other_refs, out_ref = refs[:-1], refs[-1]
    tile = out_ref.shape[1]
    sums = gathered_ref[0].astype(jnp.float32), other_refs[0][...].astype(jnp.float32)
    for k in range(1, NEAR):
        sums = sums[0] + gathered_ref[k].astype(jnp.float32), sums[1]
    for ref in other_refs[1:]:
        sums = sums[0], sums[1] + ref[...].astype(jnp.float32)
    for i, total in enumerate(sums):
        for p in range(out_ref.shape[0] // CORES):
            at = p * CORES + (place_ref[0] ^ i)
            out_ref[at] = total[p * tile : (p + 1) * tile].astype(out_ref.dtype)


def added(place, tile, gathered, others):
    steps = 4
    rows, examples = others[0].shape
    return pl.pallas_call(
        add,
        grid_spec=pltpu.PrefetchScalarGridSpec(
            num_scalar_prefetch=1,
            grid=(steps,),
            in_specs=[pl.BlockSpec((NEAR, rows // steps, examples), lambda s, place_ref: (0, s, 0))]
            + [pl.BlockSpec((rows // steps, examples), lambda s, place_ref: (s, 0))] * len(others),
            out_specs=pl.BlockSpec(
                (PAIRS * CORES // steps, tile, examples), lambda s, place_ref: (s, 0, 0)
            ),
        ),
        out_shape=jax.ShapeDtypeStruct((PAIRS * CORES, tile, examples), jnp.bfloat16),
        compiler_params=pltpu.CompilerParams(vmem_limit_bytes=16 * MIB),
        cost_estimate=pl.CostEstimate(
            flops=2 * NEAR * rows * examples,
            bytes_accessed=6 * NEAR * rows * examples,
            transcendentals=0,
        ),
    )(place, gathered, *others)


def shards(query_grads, precond, codes, scales):
    own_queries, width = query_grads.shape
    examples = codes.shape[0]
    ex_size, slots = lax.axis_size("ex"), lax.axis_size("dim")
    tile = own_queries * ex_size // slots // CORES
    chips = ROWS_X * ROWS_Y
    position = lax.axis_index("ex")
    near_here = lax.axis_index("dim") % NEAR
    place = jnp.stack([position % CORES, near_here])
    spots = [(x, y, c) for x in range(ROWS_X) for y in range(ROWS_Y) for c in range(CORES)]

    def shift(x_by, y_by, core_by):
        return [
            (e, ((x + x_by) % ROWS_X * ROWS_Y + (y + y_by) % ROWS_Y) * CORES + (c + core_by) % CORES)
            for e, (x, y, c) in enumerate(spots)
        ]

    chip_group = ROWS_Y * CORES
    beside = [list(range(x * chip_group, (x + 1) * chip_group)) for x in range(ROWS_X)]
    same_core = [[chip * CORES + c for chip in range(chips)] for c in range(CORES)]
    near = [[pair * NEAR + i for i in range(NEAR)] for pair in range(PAIRS)]
    far = [
        [(chip * CORES + c) * slots + pair * NEAR + i for pair in range(PAIRS) for c in range(CORES)]
        for chip in range(chips)
        for i in range(NEAR)
    ]

    own, halves = precond[0], spread(query_grads, tile)
    own_other = lax.ppermute(own, "ex", shift(0, 0, 1))
    across = lax.ppermute(own, "ex", shift(1, 0, 0))
    mine = dequantized(codes, scales)
    across, mine = lax.optimization_barrier((across, mine))
    across_other = lax.ppermute(across, "ex", shift(0, 0, 1))

    grads = lax.all_to_all(
        halves, "ex", 0, 0, tiled=True, axis_index_groups=beside
    ).reshape(ROWS_Y * CORES * 2 * tile, width)

    grads, mine, own_other, across, across_other = lax.optimization_barrier(
        (grads, mine, own_other, across, across_other)
    )
    copies = conditioned_for(place, chips, grads, [own, own_other, across, across_other])
    mine, copies = lax.optimization_barrier((mine, copies))
    theirs = lax.ppermute(mine, "ex", shift(0, 0, 1))
    parts = lax.all_to_all(copies, "ex", 0, 0, tiled=True, axis_index_groups=same_core)

    terms, here, away = scores_of(place, parts, mine, theirs)
    gathered = lax.all_to_all(terms, "dim", 0, 0, tiled=True, axis_index_groups=near)
    came = lax.ppermute(
        away, "dim", [(d, (((d + SIDES) ^ SIDES) - SIDES) % slots) for d in range(slots)]
    )
    kept, sent = folded(here, came)
    others = [kept, lax.ppermute(sent, "dim", [(d, d ^ 1) for d in range(slots)])]
    sums = lax.all_to_all(
        added(place, tile, gathered, others), ("ex", "dim"), 0, 0, tiled=True, axis_index_groups=far
    )
    total = jnp.sum(sums.astype(jnp.float32).reshape(PAIRS, CORES * tile, examples), axis=0)
    return total * float(width * slots) ** (-0.5)


def solution(mesh):
    placed = (P("ex", "dim"), P("dim", None, "ex"), P("ex", "dim"), P("ex", "dim"))
    return jax.shard_map(
        shards, mesh=mesh, in_specs=placed, out_specs=P("dim", "ex"), check_vma=False
    )
```

```python
import functools

import jax
import jax.numpy as jnp
from jax import lax
from jax.experimental import pallas as pl
from jax.experimental.pallas import tpu as pltpu
from jax.sharding import PartitionSpec as P

CORES, ROWS_Y, ROWS_X = 2, 4, 2
PAIRS, SIDES = 8, 2
NEAR = 2 * SIDES
MIB = 1 << 20


def dequantize(codes_ref, scales_ref, out_ref):
    block = codes_ref.shape[1] // scales_ref.shape[1]
    for b in range(scales_ref.shape[1]):
        columns = slice(b * block, (b + 1) * block)
        entries = codes_ref[:, columns].astype(jnp.float32) * scales_ref[:, b : b + 1]
        out_ref[:, columns] = entries.astype(out_ref.dtype)


def dequantized(codes, scales):
    rows, width = codes.shape
    tile = 256
    return pl.pallas_call(
        dequantize,
        grid=(rows // tile,),
        in_specs=[
            pl.BlockSpec((tile, width), lambda r: (r, 0)),
            pl.BlockSpec((tile, scales.shape[1]), lambda r: (r, 0)),
        ],
        out_specs=pl.BlockSpec((tile, width), lambda r: (r, 0)),
        out_shape=jax.ShapeDtypeStruct(codes.shape, jnp.bfloat16),
        compiler_params=pltpu.CompilerParams(vmem_limit_bytes=56 * MIB),
        cost_estimate=pl.CostEstimate(
            flops=rows * width, bytes_accessed=4 * rows * width, transcendentals=0
        ),
    )(codes, scales)


def copy_halves(grads_ref, out_ref):
    tile = out_ref.shape[1] // 2
    for b in range(2):
        for core in range(CORES):
            row = (b * CORES + core) * tile
            entries = grads_ref[row : row + tile, :]
            for y in range(ROWS_Y):
                out_ref[y * CORES + core, b * tile : (b + 1) * tile, :] = entries


def spread(grads, tile):
    rows, width = grads.shape
    return pl.pallas_call(
        copy_halves,
        in_specs=[pl.BlockSpec(memory_space=pltpu.VMEM)],
        out_specs=pl.BlockSpec(memory_space=pltpu.VMEM),
        out_shape=jax.ShapeDtypeStruct((ROWS_Y * CORES, 2 * tile, width), grads.dtype),
        compiler_params=pltpu.CompilerParams(vmem_limit_bytes=8 * MIB),
        cost_estimate=pl.CostEstimate(
            flops=0, bytes_accessed=2 * (1 + ROWS_Y) * rows * width, transcendentals=0
        ),
    )(grads)


def condition(place_ref, *refs):
    grads_ref, column_refs, (parts_ref, weights) = refs[0], refs[1:-2], refs[-2:]
    columns = column_refs[0].shape[1]
    for core in range(CORES):

        @pl.when(place_ref[0] == core)
        def _():
            for i, ref in enumerate(column_refs):
                at = (i ^ core) * columns
                weights[:, at : at + columns] = ref[...]

    part = jnp.dot(grads_ref[...], weights[...], preferred_element_type=jnp.float32)
    for chip in range(parts_ref.shape[0]):
        parts_ref[chip] = part.astype(parts_ref.dtype)


def conditioned_for(place, chips, grads, columns):
    rows, width = grads.shape
    out = len(columns) * columns[0].shape[1]
    return pl.pallas_call(
        condition,
        in_specs=[pl.BlockSpec(memory_space=pltpu.SMEM)]
        + [pl.BlockSpec(memory_space=pltpu.VMEM)] * (1 + len(columns)),
        out_specs=pl.BlockSpec(memory_space=pltpu.VMEM),
        out_shape=jax.ShapeDtypeStruct((chips, rows, out), jnp.bfloat16),
        scratch_shapes=[pltpu.VMEM((width, out), jnp.bfloat16)],
        compiler_params=pltpu.CompilerParams(vmem_limit_bytes=16 * MIB),
        cost_estimate=pl.CostEstimate(
            flops=2 * rows * width * out,
            bytes_accessed=2 * (rows * width + width * out + chips * rows * out),
            transcendentals=0,
        ),
    )(place, grads, *columns)


def score(apart, place_ref, parts_ref, store_ref, *refs):
    out_refs, queries = refs[:-1], refs[-1]
    block_rows, columns = parts_ref.shape[1], parts_ref.shape[2] // ROWS_X
    rows = block_rows // ROWS_Y
    tile = rows // NEAR

    @pl.when(pl.program_id(0) == 0)
    def _():
        for x in range(ROWS_X):
            for pair in range(ROWS_Y):
                for near in range(NEAR):
                    to = (x * ROWS_Y + pair) * tile
                    if apart:
                        to = pl.multiple_of((near ^ place_ref[1]) * (PAIRS * tile) + to, tile)
                    else:
                        to += near * PAIRS * tile
                    row = pair * rows + near * tile
                    for y in range(ROWS_Y):
                        for k in range(ROWS_X):
                            at = ((x ^ k) * ROWS_Y + y) * columns
                            queries[pl.ds(to, tile), at : at + columns] = parts_ref[
                                x * ROWS_Y + y, row : row + tile, k * columns : (k + 1) * columns
                            ]

    term = lax.dot_general(
        queries[...], store_ref[...], (((1,), (1,)), ((), ())),
        preferred_element_type=jnp.float32,
    )
    for k in range(NEAR):
        entries = term[k * PAIRS * tile : (k + 1) * PAIRS * tile].astype(out_refs[0].dtype)
        if apart:
            out_refs[k][...] = entries
        else:
            out_refs[0][k] = entries


def scores_of(apart, place, parts, store):
    chips, block_rows, columns = parts.shape
    rows = ROWS_X * block_rows
    examples, width = store.shape
    tile = 256
    if apart:
        block, index, shape, count = (rows // NEAR, tile), lambda n, place_ref: (0, n), (rows // NEAR, examples), NEAR
    else:
        block, index = (NEAR, rows // NEAR, tile), lambda n, place_ref: (0, 0, n)
        shape, count = (NEAR, rows // NEAR, examples), 1
    return pl.pallas_call(
        functools.partial(score, apart),
        grid_spec=pltpu.PrefetchScalarGridSpec(
            num_scalar_prefetch=1,
            grid=(examples // tile,),
            in_specs=[
                pl.BlockSpec((chips, block_rows, columns), lambda n, place_ref: (0, 0, 0)),
                pl.BlockSpec((tile, width), lambda n, place_ref: (n, 0)),
            ],
            out_specs=[pl.BlockSpec(block, index)] * count,
            scratch_shapes=[pltpu.VMEM((rows, width), jnp.bfloat16)],
        ),
        out_shape=[jax.ShapeDtypeStruct(shape, jnp.bfloat16) if apart else pltpu.HBM(shape, jnp.bfloat16)] * count,
        compiler_params=pltpu.CompilerParams(vmem_limit_bytes=50 * MIB),
        cost_estimate=pl.CostEstimate(
            flops=2 * rows * width * examples,
            bytes_accessed=2 * (rows * width + (width + rows) * examples),
            transcendentals=0,
        ),
    )(place, parts, store)


def add(place_ref, gathered_ref, *refs):
    other_refs, out_ref = refs[:-1], refs[-1]
    tile = out_ref.shape[1]
    sums = gathered_ref[0].astype(jnp.float32), other_refs[0][...].astype(jnp.float32)
    for k in range(1, NEAR):
        sums = (
            sums[0] + gathered_ref[k].astype(jnp.float32),
            sums[1] + other_refs[k][...].astype(jnp.float32),
        )
    for i, total in enumerate(sums):
        for p in range(out_ref.shape[0] // CORES):
            at = p * CORES + (place_ref[0] ^ i)
            out_ref[at] = total[p * tile : (p + 1) * tile].astype(out_ref.dtype)


def added(place, tile, gathered, others):
    steps = 4
    rows, examples = others[0].shape
    return pl.pallas_call(
        add,
        grid_spec=pltpu.PrefetchScalarGridSpec(
            num_scalar_prefetch=1,
            grid=(steps,),
            in_specs=[pl.BlockSpec((NEAR, rows // steps, examples), lambda s, place_ref: (0, s, 0))]
            + [pl.BlockSpec((rows // steps, examples), lambda s, place_ref: (s, 0))] * NEAR,
            out_specs=pl.BlockSpec(
                (PAIRS * CORES // steps, tile, examples), lambda s, place_ref: (s, 0, 0)
            ),
        ),
        out_shape=jax.ShapeDtypeStruct((PAIRS * CORES, tile, examples), jnp.bfloat16),
        compiler_params=pltpu.CompilerParams(vmem_limit_bytes=16 * MIB),
        cost_estimate=pl.CostEstimate(
            flops=2 * NEAR * rows * examples,
            bytes_accessed=6 * NEAR * rows * examples,
            transcendentals=0,
        ),
    )(place, gathered, *others)


def shards(query_grads, precond, codes, scales):
    own_queries, width = query_grads.shape
    examples = codes.shape[0]
    ex_size, slots = lax.axis_size("ex"), lax.axis_size("dim")
    tile = own_queries * ex_size // slots // CORES
    chips = ROWS_X * ROWS_Y
    position = lax.axis_index("ex")
    near_here = lax.axis_index("dim") % NEAR
    place = jnp.stack([position % CORES, near_here])
    spots = [(x, y, c) for x in range(ROWS_X) for y in range(ROWS_Y) for c in range(CORES)]

    def shift(x_by, y_by, core_by):
        return [
            (e, ((x + x_by) % ROWS_X * ROWS_Y + (y + y_by) % ROWS_Y) * CORES + (c + core_by) % CORES)
            for e, (x, y, c) in enumerate(spots)
        ]

    chip_group = ROWS_Y * CORES
    beside = [list(range(x * chip_group, (x + 1) * chip_group)) for x in range(ROWS_X)]
    same_core = [[chip * CORES + c for chip in range(chips)] for c in range(CORES)]
    near = [[pair * NEAR + i for i in range(NEAR)] for pair in range(PAIRS)]
    far = [
        [(chip * CORES + c) * slots + pair * NEAR + i for pair in range(PAIRS) for c in range(CORES)]
        for chip in range(chips)
        for i in range(NEAR)
    ]

    own, halves = precond[0], spread(query_grads, tile)
    own_other = lax.ppermute(own, "ex", shift(0, 0, 1))
    across = lax.ppermute(own, "ex", shift(1, 0, 0))
    mine = dequantized(codes, scales)
    across, mine = lax.optimization_barrier((across, mine))
    across_other = lax.ppermute(across, "ex", shift(0, 0, 1))

    grads = lax.all_to_all(
        halves, "ex", 0, 0, tiled=True, axis_index_groups=beside
    ).reshape(ROWS_Y * CORES * 2 * tile, width)

    grads, mine, own_other, across, across_other = lax.optimization_barrier(
        (grads, mine, own_other, across, across_other)
    )
    copies = conditioned_for(place, chips, grads, [own, own_other, across, across_other])
    mine, copies = lax.optimization_barrier((mine, copies))
    theirs = lax.ppermute(mine, "ex", shift(0, 0, 1))
    parts = lax.all_to_all(copies, "ex", 0, 0, tiled=True, axis_index_groups=same_core)

    (terms,) = scores_of(False, place, parts, mine)
    gathered = lax.all_to_all(terms, "dim", 0, 0, tiled=True, axis_index_groups=near)
    here, *away = scores_of(True, place, parts, theirs)
    others = [here]
    for k in (1, 3, 2):
        swap = [(d, (((d + SIDES) ^ k) - SIDES) % slots if k & SIDES else d ^ k) for d in range(slots)]
        others.append(lax.ppermute(away[k - 1], "dim", swap))
    sums = lax.all_to_all(
        added(place, tile, gathered, others), ("ex", "dim"), 0, 0, tiled=True, axis_index_groups=far
    )
    total = jnp.sum(sums.astype(jnp.float32).reshape(PAIRS, CORES * tile, examples), axis=0)
    return total * float(width * slots) ** (-0.5)


def solution(mesh):
    placed = (P("ex", "dim"), P("dim", None, "ex"), P("ex", "dim"), P("ex", "dim"))
    return jax.shard_map(
        shards, mesh=mesh, in_specs=placed, out_specs=P("dim", "ex"), check_vma=False
    )
```

```python
import functools

import jax
import jax.numpy as jnp
from jax import lax
from jax.experimental import pallas as pl
from jax.experimental.pallas import tpu as pltpu
from jax.sharding import PartitionSpec as P

CORES, ROWS_Y, ROWS_X = 2, 4, 2
PAIRS, SIDES = 8, 2
NEAR = 2 * SIDES
MIB = 1 << 20


def dequantize(codes_ref, scales_ref, out_ref):
    block = codes_ref.shape[1] // scales_ref.shape[1]
    for b in range(scales_ref.shape[1]):
        columns = slice(b * block, (b + 1) * block)
        entries = codes_ref[:, columns].astype(jnp.float32) * scales_ref[:, b : b + 1]
        out_ref[:, columns] = entries.astype(out_ref.dtype)


def dequantized(codes, scales):
    rows, width = codes.shape
    tile = 256
    return pl.pallas_call(
        dequantize,
        grid=(rows // tile,),
        in_specs=[
            pl.BlockSpec((tile, width), lambda r: (r, 0)),
            pl.BlockSpec((tile, scales.shape[1]), lambda r: (r, 0)),
        ],
        out_specs=pl.BlockSpec((tile, width), lambda r: (r, 0)),
        out_shape=jax.ShapeDtypeStruct(codes.shape, jnp.bfloat16),
        compiler_params=pltpu.CompilerParams(vmem_limit_bytes=56 * MIB),
        cost_estimate=pl.CostEstimate(
            flops=rows * width, bytes_accessed=4 * rows * width, transcendentals=0
        ),
    )(codes, scales)


def copy_halves(grads_ref, out_ref):
    tile = out_ref.shape[1] // 2
    for b in range(2):
        for core in range(CORES):
            row = (b * CORES + core) * tile
            entries = grads_ref[row : row + tile, :]
            for y in range(ROWS_Y):
                out_ref[y * CORES + core, b * tile : (b + 1) * tile, :] = entries


def spread(grads, tile):
    rows, width = grads.shape
    return pl.pallas_call(
        copy_halves,
        in_specs=[pl.BlockSpec(memory_space=pltpu.VMEM)],
        out_specs=pl.BlockSpec(memory_space=pltpu.VMEM),
        out_shape=jax.ShapeDtypeStruct((ROWS_Y * CORES, 2 * tile, width), grads.dtype),
        compiler_params=pltpu.CompilerParams(vmem_limit_bytes=8 * MIB),
        cost_estimate=pl.CostEstimate(
            flops=0, bytes_accessed=2 * (1 + ROWS_Y) * rows * width, transcendentals=0
        ),
    )(grads)


def condition(place_ref, *refs):
    grads_ref, column_refs, (parts_ref, weights) = refs[0], refs[1:-2], refs[-2:]
    columns = column_refs[0].shape[1]
    for core in range(CORES):

        @pl.when(place_ref[0] == core)
        def _():
            for i, ref in enumerate(column_refs):
                at = (i ^ core) * columns
                weights[:, at : at + columns] = ref[...]

    part = jnp.dot(grads_ref[...], weights[...], preferred_element_type=jnp.float32)
    for chip in range(parts_ref.shape[0]):
        parts_ref[chip] = part.astype(parts_ref.dtype)


def conditioned_for(place, chips, grads, columns):
    rows, width = grads.shape
    out = len(columns) * columns[0].shape[1]
    return pl.pallas_call(
        condition,
        in_specs=[pl.BlockSpec(memory_space=pltpu.SMEM)]
        + [pl.BlockSpec(memory_space=pltpu.VMEM)] * (1 + len(columns)),
        out_specs=pl.BlockSpec(memory_space=pltpu.VMEM),
        out_shape=jax.ShapeDtypeStruct((chips, rows, out), jnp.bfloat16),
        scratch_shapes=[pltpu.VMEM((width, out), jnp.bfloat16)],
        compiler_params=pltpu.CompilerParams(vmem_limit_bytes=16 * MIB),
        cost_estimate=pl.CostEstimate(
            flops=2 * rows * width * out,
            bytes_accessed=2 * (rows * width + width * out + chips * rows * out),
            transcendentals=0,
        ),
    )(place, grads, *columns)


def score(apart, place_ref, parts_ref, store_ref, *refs):
    out_refs, queries = refs[:-1], refs[-1]
    block_rows, columns = parts_ref.shape[1], parts_ref.shape[2] // ROWS_X
    rows = block_rows // ROWS_Y
    tile = rows // NEAR

    @pl.when(pl.program_id(0) == 0)
    def _():
        for x in range(ROWS_X):
            for pair in range(ROWS_Y):
                for near in range(NEAR):
                    to = (x * ROWS_Y + pair) * tile
                    if apart:
                        to = pl.multiple_of((near ^ place_ref[1]) * (PAIRS * tile) + to, tile)
                    else:
                        to += near * PAIRS * tile
                    row = pair * rows + near * tile
                    for y in range(ROWS_Y):
                        for k in range(ROWS_X):
                            at = ((x ^ k) * ROWS_Y + y) * columns
                            queries[pl.ds(to, tile), at : at + columns] = parts_ref[
                                x * ROWS_Y + y, row : row + tile, k * columns : (k + 1) * columns
                            ]

    term = lax.dot_general(
        queries[...], store_ref[...], (((1,), (1,)), ((), ())),
        preferred_element_type=jnp.float32,
    )
    for k in range(NEAR):
        entries = term[k * PAIRS * tile : (k + 1) * PAIRS * tile].astype(out_refs[0].dtype)
        if apart:
            out_refs[k][...] = entries
        else:
            out_refs[0][k] = entries


def scores_of(apart, place, parts, store):
    chips, block_rows, columns = parts.shape
    rows = ROWS_X * block_rows
    examples, width = store.shape
    tile = 512
    if apart:
        block, index, shape, count = (rows // NEAR, tile), lambda n, place_ref: (0, n), (rows // NEAR, examples), NEAR
    else:
        block, index = (NEAR, rows // NEAR, tile), lambda n, place_ref: (0, 0, n)
        shape, count = (NEAR, rows // NEAR, examples), 1
    return pl.pallas_call(
        functools.partial(score, apart),
        grid_spec=pltpu.PrefetchScalarGridSpec(
            num_scalar_prefetch=1,
            grid=(examples // tile,),
            in_specs=[
                pl.BlockSpec((chips, block_rows, columns), lambda n, place_ref: (0, 0, 0)),
                pl.BlockSpec((tile, width), lambda n, place_ref: (n, 0)),
            ],
            out_specs=[pl.BlockSpec(block, index)] * count,
            scratch_shapes=[pltpu.VMEM((rows, width), jnp.bfloat16)],
        ),
        out_shape=[jax.ShapeDtypeStruct(shape, jnp.bfloat16) if apart else pltpu.HBM(shape, jnp.bfloat16)] * count,
        compiler_params=pltpu.CompilerParams(vmem_limit_bytes=50 * MIB),
        cost_estimate=pl.CostEstimate(
            flops=2 * rows * width * examples,
            bytes_accessed=2 * (rows * width + (width + rows) * examples),
            transcendentals=0,
        ),
    )(place, parts, store)


def add(place_ref, gathered_ref, *refs):
    other_refs, out_ref = refs[:-1], refs[-1]
    tile = out_ref.shape[1]
    sums = gathered_ref[0].astype(jnp.float32), other_refs[0][...].astype(jnp.float32)
    for k in range(1, NEAR):
        sums = (
            sums[0] + gathered_ref[k].astype(jnp.float32),
            sums[1] + other_refs[k][...].astype(jnp.float32),
        )
    for i, total in enumerate(sums):
        for p in range(out_ref.shape[0] // CORES):
            at = p * CORES + (place_ref[0] ^ i)
            out_ref[at] = total[p * tile : (p + 1) * tile].astype(out_ref.dtype)


def added(place, tile, gathered, others):
    steps = 4
    rows, examples = others[0].shape
    return pl.pallas_call(
        add,
        grid_spec=pltpu.PrefetchScalarGridSpec(
            num_scalar_prefetch=1,
            grid=(steps,),
            in_specs=[pl.BlockSpec((NEAR, rows // steps, examples), lambda s, place_ref: (0, s, 0))]
            + [pl.BlockSpec((rows // steps, examples), lambda s, place_ref: (s, 0))] * NEAR,
            out_specs=pl.BlockSpec(
                (PAIRS * CORES // steps, tile, examples), lambda s, place_ref: (s, 0, 0)
            ),
        ),
        out_shape=jax.ShapeDtypeStruct((PAIRS * CORES, tile, examples), jnp.bfloat16),
        compiler_params=pltpu.CompilerParams(vmem_limit_bytes=16 * MIB),
        cost_estimate=pl.CostEstimate(
            flops=2 * NEAR * rows * examples,
            bytes_accessed=6 * NEAR * rows * examples,
            transcendentals=0,
        ),
    )(place, gathered, *others)


def shards(query_grads, precond, codes, scales):
    own_queries, width = query_grads.shape
    examples = codes.shape[0]
    ex_size, slots = lax.axis_size("ex"), lax.axis_size("dim")
    tile = own_queries * ex_size // slots // CORES
    chips = ROWS_X * ROWS_Y
    position = lax.axis_index("ex")
    near_here = lax.axis_index("dim") % NEAR
    place = jnp.stack([position % CORES, near_here])
    spots = [(x, y, c) for x in range(ROWS_X) for y in range(ROWS_Y) for c in range(CORES)]

    def shift(x_by, y_by, core_by):
        return [
            (e, ((x + x_by) % ROWS_X * ROWS_Y + (y + y_by) % ROWS_Y) * CORES + (c + core_by) % CORES)
            for e, (x, y, c) in enumerate(spots)
        ]

    chip_group = ROWS_Y * CORES
    beside = [list(range(x * chip_group, (x + 1) * chip_group)) for x in range(ROWS_X)]
    same_core = [[chip * CORES + c for chip in range(chips)] for c in range(CORES)]
    near = [[pair * NEAR + i for i in range(NEAR)] for pair in range(PAIRS)]
    far = [
        [(chip * CORES + c) * slots + pair * NEAR + i for pair in range(PAIRS) for c in range(CORES)]
        for chip in range(chips)
        for i in range(NEAR)
    ]

    own, halves = precond[0], spread(query_grads, tile)
    own_other = lax.ppermute(own, "ex", shift(0, 0, 1))
    across = lax.ppermute(own, "ex", shift(1, 0, 0))
    mine = dequantized(codes, scales)
    across, mine = lax.optimization_barrier((across, mine))
    across_other = lax.ppermute(across, "ex", shift(0, 0, 1))

    grads = lax.all_to_all(
        halves, "ex", 0, 0, tiled=True, axis_index_groups=beside
    ).reshape(ROWS_Y * CORES * 2 * tile, width)

    grads, mine, own_other, across, across_other = lax.optimization_barrier(
        (grads, mine, own_other, across, across_other)
    )
    copies = conditioned_for(place, chips, grads, [own, own_other, across, across_other])
    mine, copies = lax.optimization_barrier((mine, copies))
    theirs = lax.ppermute(mine, "ex", shift(0, 0, 1))
    parts = lax.all_to_all(copies, "ex", 0, 0, tiled=True, axis_index_groups=same_core)

    (terms,) = scores_of(False, place, parts, mine)
    gathered = lax.all_to_all(terms, "dim", 0, 0, tiled=True, axis_index_groups=near)
    here, *away = scores_of(True, place, parts, theirs)
    others = [here] + [
        lax.ppermute(
            term, "dim", [(d, (((d + SIDES) ^ k) - SIDES) % slots if k & SIDES else d ^ k) for d in range(slots)]
        )
        for k, term in enumerate(away, 1)
    ]
    sums = lax.all_to_all(
        added(place, tile, gathered, others), ("ex", "dim"), 0, 0, tiled=True, axis_index_groups=far
    )
    total = jnp.sum(sums.astype(jnp.float32).reshape(PAIRS, CORES * tile, examples), axis=0)
    return total * float(width * slots) ** (-0.5)


def solution(mesh):
    placed = (P("ex", "dim"), P("dim", None, "ex"), P("ex", "dim"), P("ex", "dim"))
    return jax.shard_map(
        shards, mesh=mesh, in_specs=placed, out_specs=P("dim", "ex"), check_vma=False
    )
```

```python
import functools

import jax
import jax.numpy as jnp
from jax import lax
from jax.experimental import pallas as pl
from jax.experimental.pallas import tpu as pltpu
from jax.sharding import PartitionSpec as P

CORES, ROWS_Y, ROWS_X = 2, 4, 2
PAIRS, SIDES = 8, 2
NEAR = 2 * SIDES
MIB = 1 << 20


def dequantize(codes_ref, scales_ref, out_ref):
    block = codes_ref.shape[1] // scales_ref.shape[1]
    for b in range(scales_ref.shape[1]):
        columns = slice(b * block, (b + 1) * block)
        entries = codes_ref[:, columns].astype(jnp.float32) * scales_ref[:, b : b + 1]
        out_ref[:, columns] = entries.astype(out_ref.dtype)


def dequantized(codes, scales):
    rows, width = codes.shape
    tile = 256
    return pl.pallas_call(
        dequantize,
        grid=(rows // tile,),
        in_specs=[
            pl.BlockSpec((tile, width), lambda r: (r, 0)),
            pl.BlockSpec((tile, scales.shape[1]), lambda r: (r, 0)),
        ],
        out_specs=pl.BlockSpec((tile, width), lambda r: (r, 0)),
        out_shape=jax.ShapeDtypeStruct(codes.shape, jnp.bfloat16),
        compiler_params=pltpu.CompilerParams(vmem_limit_bytes=56 * MIB),
        cost_estimate=pl.CostEstimate(
            flops=rows * width, bytes_accessed=4 * rows * width, transcendentals=0
        ),
    )(codes, scales)


def copy_halves(grads_ref, out_ref):
    tile = out_ref.shape[1]
    for core in range(CORES):
        entries = grads_ref[core * tile : (core + 1) * tile, :]
        for y in range(ROWS_Y):
            out_ref[y * CORES + core] = entries


def spread(grads, tile):
    rows, width = grads.shape
    return pl.pallas_call(
        copy_halves,
        grid=(2,),
        in_specs=[pl.BlockSpec((CORES * tile, width), lambda b: (b, 0))],
        out_specs=pl.BlockSpec((ROWS_Y * CORES, tile, width), lambda b: (0, b, 0)),
        out_shape=pltpu.HBM((ROWS_Y * CORES, 2 * tile, width), grads.dtype),
        compiler_params=pltpu.CompilerParams(vmem_limit_bytes=60 * MIB),
        cost_estimate=pl.CostEstimate(
            flops=0, bytes_accessed=2 * (1 + ROWS_Y) * rows * width, transcendentals=0
        ),
    )(grads)


def condition(place_ref, *refs):
    grads_ref, column_refs, (parts_ref, weights) = refs[0], refs[1:-2], refs[-2:]
    columns = column_refs[0].shape[1]
    for core in range(CORES):

        @pl.when(place_ref[0] == core)
        def _():
            for i, ref in enumerate(column_refs):
                at = (i ^ core) * columns
                weights[:, at : at + columns] = ref[...]

    part = jnp.dot(grads_ref[...], weights[...], preferred_element_type=jnp.float32)
    for chip in range(parts_ref.shape[0]):
        parts_ref[chip] = part.astype(parts_ref.dtype)


def conditioned_for(place, chips, grads, columns):
    rows, width = grads.shape
    out = len(columns) * columns[0].shape[1]
    return pl.pallas_call(
        condition,
        in_specs=[pl.BlockSpec(memory_space=pltpu.SMEM)]
        + [pl.BlockSpec(memory_space=pltpu.VMEM)] * (1 + len(columns)),
        out_specs=pl.BlockSpec(memory_space=pltpu.VMEM),
        out_shape=jax.ShapeDtypeStruct((chips, rows, out), jnp.bfloat16),
        scratch_shapes=[pltpu.VMEM((width, out), jnp.bfloat16)],
        compiler_params=pltpu.CompilerParams(vmem_limit_bytes=16 * MIB),
        cost_estimate=pl.CostEstimate(
            flops=2 * rows * width * out,
            bytes_accessed=2 * (rows * width + width * out + chips * rows * out),
            transcendentals=0,
        ),
    )(place, grads, *columns)


def score(apart, place_ref, parts_ref, store_ref, *refs):
    out_refs, queries = refs[:-1], refs[-1]
    block_rows, columns = parts_ref.shape[1], parts_ref.shape[2] // ROWS_X
    rows = block_rows // ROWS_Y
    tile = rows // NEAR

    @pl.when(pl.program_id(0) == 0)
    def _():
        for x in range(ROWS_X):
            for pair in range(ROWS_Y):
                for near in range(NEAR):
                    to = (x * ROWS_Y + pair) * tile
                    if apart:
                        to = pl.multiple_of((near ^ place_ref[1]) * (PAIRS * tile) + to, tile)
                    else:
                        to += near * PAIRS * tile
                    row = pair * rows + near * tile
                    for y in range(ROWS_Y):
                        for k in range(ROWS_X):
                            at = ((x ^ k) * ROWS_Y + y) * columns
                            queries[pl.ds(to, tile), at : at + columns] = parts_ref[
                                x * ROWS_Y + y, row : row + tile, k * columns : (k + 1) * columns
                            ]

    term = lax.dot_general(
        queries[...], store_ref[...], (((1,), (1,)), ((), ())),
        preferred_element_type=jnp.float32,
    )
    for k in range(NEAR):
        entries = term[k * PAIRS * tile : (k + 1) * PAIRS * tile].astype(out_refs[0].dtype)
        if apart:
            out_refs[k][...] = entries
        else:
            out_refs[0][k] = entries


def scores_of(apart, place, parts, store):
    chips, block_rows, columns = parts.shape
    rows = ROWS_X * block_rows
    examples, width = store.shape
    tile = 512
    if apart:
        block, index, shape, count = (rows // NEAR, tile), lambda n, place_ref: (0, n), (rows // NEAR, examples), NEAR
    else:
        block, index = (NEAR, rows // NEAR, tile), lambda n, place_ref: (0, 0, n)
        shape, count = (NEAR, rows // NEAR, examples), 1
    return pl.pallas_call(
        functools.partial(score, apart),
        grid_spec=pltpu.PrefetchScalarGridSpec(
            num_scalar_prefetch=1,
            grid=(examples // tile,),
            in_specs=[
                pl.BlockSpec((chips, block_rows, columns), lambda n, place_ref: (0, 0, 0)),
                pl.BlockSpec((tile, width), lambda n, place_ref: (n, 0)),
            ],
            out_specs=[pl.BlockSpec(block, index)] * count,
            scratch_shapes=[pltpu.VMEM((rows, width), jnp.bfloat16)],
        ),
        out_shape=[jax.ShapeDtypeStruct(shape, jnp.bfloat16) if apart else pltpu.HBM(shape, jnp.bfloat16)] * count,
        compiler_params=pltpu.CompilerParams(vmem_limit_bytes=50 * MIB),
        cost_estimate=pl.CostEstimate(
            flops=2 * rows * width * examples,
            bytes_accessed=2 * (rows * width + (width + rows) * examples),
            transcendentals=0,
        ),
    )(place, parts, store)


def add(place_ref, gathered_ref, *refs):
    other_refs, out_ref = refs[:-1], refs[-1]
    tile = out_ref.shape[1]
    sums = gathered_ref[0].astype(jnp.float32), other_refs[0][...].astype(jnp.float32)
    for k in range(1, NEAR):
        sums = (
            sums[0] + gathered_ref[k].astype(jnp.float32),
            sums[1] + other_refs[k][...].astype(jnp.float32),
        )
    for i, total in enumerate(sums):
        for p in range(out_ref.shape[0] // CORES):
            at = p * CORES + (place_ref[0] ^ i)
            out_ref[at] = total[p * tile : (p + 1) * tile].astype(out_ref.dtype)


def added(place, tile, gathered, others):
    steps = 4
    rows, examples = others[0].shape
    return pl.pallas_call(
        add,
        grid_spec=pltpu.PrefetchScalarGridSpec(
            num_scalar_prefetch=1,
            grid=(steps,),
            in_specs=[pl.BlockSpec((NEAR, rows // steps, examples), lambda s, place_ref: (0, s, 0))]
            + [pl.BlockSpec((rows // steps, examples), lambda s, place_ref: (s, 0))] * NEAR,
            out_specs=pl.BlockSpec(
                (PAIRS * CORES // steps, tile, examples), lambda s, place_ref: (s, 0, 0)
            ),
        ),
        out_shape=jax.ShapeDtypeStruct((PAIRS * CORES, tile, examples), jnp.bfloat16),
        compiler_params=pltpu.CompilerParams(vmem_limit_bytes=16 * MIB),
        cost_estimate=pl.CostEstimate(
            flops=2 * NEAR * rows * examples,
            bytes_accessed=6 * NEAR * rows * examples,
            transcendentals=0,
        ),
    )(place, gathered, *others)


def shards(query_grads, precond, codes, scales):
    own_queries, width = query_grads.shape
    examples = codes.shape[0]
    ex_size, slots = lax.axis_size("ex"), lax.axis_size("dim")
    tile = own_queries * ex_size // slots // CORES
    chips = ROWS_X * ROWS_Y
    position = lax.axis_index("ex")
    near_here = lax.axis_index("dim") % NEAR
    place = jnp.stack([position % CORES, near_here])
    spots = [(x, y, c) for x in range(ROWS_X) for y in range(ROWS_Y) for c in range(CORES)]

    def shift(x_by, y_by, core_by):
        return [
            (e, ((x + x_by) % ROWS_X * ROWS_Y + (y + y_by) % ROWS_Y) * CORES + (c + core_by) % CORES)
            for e, (x, y, c) in enumerate(spots)
        ]

    chip_group = ROWS_Y * CORES
    beside = [list(range(x * chip_group, (x + 1) * chip_group)) for x in range(ROWS_X)]
    same_core = [[chip * CORES + c for chip in range(chips)] for c in range(CORES)]
    near = [[pair * NEAR + i for i in range(NEAR)] for pair in range(PAIRS)]
    far = [
        [(chip * CORES + c) * slots + pair * NEAR + i for pair in range(PAIRS) for c in range(CORES)]
        for chip in range(chips)
        for i in range(NEAR)
    ]

    own, halves = precond[0], spread(query_grads, tile)
    own_other = lax.ppermute(own, "ex", shift(0, 0, 1))
    across = lax.ppermute(own, "ex", shift(1, 0, 0))
    mine = dequantized(codes, scales)
    across, mine = lax.optimization_barrier((across, mine))
    across_other = lax.ppermute(across, "ex", shift(0, 0, 1))

    grads = lax.all_to_all(
        halves, "ex", 0, 0, tiled=True, axis_index_groups=beside
    ).reshape(ROWS_Y * CORES * 2 * tile, width)

    grads, mine, own_other, across, across_other = lax.optimization_barrier(
        (grads, mine, own_other, across, across_other)
    )
    copies = conditioned_for(place, chips, grads, [own, own_other, across, across_other])
    mine, copies = lax.optimization_barrier((mine, copies))
    theirs = lax.ppermute(mine, "ex", shift(0, 0, 1))
    parts = lax.all_to_all(copies, "ex", 0, 0, tiled=True, axis_index_groups=same_core)

    (terms,) = scores_of(False, place, parts, mine)
    gathered = lax.all_to_all(terms, "dim", 0, 0, tiled=True, axis_index_groups=near)
    here, *away = scores_of(True, place, parts, theirs)
    others = [here] + [
        lax.ppermute(
            term, "dim", [(d, (((d + SIDES) ^ k) - SIDES) % slots if k & SIDES else d ^ k) for d in range(slots)]
        )
        for k, term in enumerate(away, 1)
    ]
    sums = lax.all_to_all(
        added(place, tile, gathered, others), ("ex", "dim"), 0, 0, tiled=True, axis_index_groups=far
    )
    total = jnp.sum(sums.astype(jnp.float32).reshape(PAIRS, CORES * tile, examples), axis=0)
    return total * float(width * slots) ** (-0.5)


def solution(mesh):
    placed = (P("ex", "dim"), P("dim", None, "ex"), P("ex", "dim"), P("ex", "dim"))
    return jax.shard_map(
        shards, mesh=mesh, in_specs=placed, out_specs=P("dim", "ex"), check_vma=False
    )
```
